512 devices in a mesh: row: 32 (over x, y), col: 16 (over z, core).
Axes of the slice: x: 4, y: 8, z: 8, core: 2. Of those that a mesh axis runs over, the one named last changes fastest.
Arguments:
- k_vals: float32 [512, 15, 64, 64], P('row'), may hold values from -0.1875 to 0.1875
- k_cols: int32 [512, 15], P('row'), may hold values from -8 to 519, as said below
- p_vals: float32 [512, 3, 64, 64], P('row', None, None, 'col'), may hold values from -1.2 to 1.2
- p_cols: int32 [512, 3], P('row'), may hold values from -1 to 63, as said below
Outputs:
- coarse: float32 [64, 7, 64, 64], P('row', None, None, 'col')
The draws below stay inside these ranges and needn't reach their ends.
Inputs may be any that keep to these rules, and one draw needn't show every extreme that they name: Each k_cols[i, s] - i lies between -8 and 8; within a block row the columns differ; a column outside 0 to 511 stands for an absent block. Each p_cols[k, s] is -1 for an absent block or lies within 1 of k // 8, the aggregate of block row k; the present columns of a row differ, and the aggregate of every block row is present.
All inputs are finite; a program needn't handle non-finite values.
Results may differ from the reference program's by a relative error of at most 0.0001.
Values sent between devices are 32-bit elements; how exact they have to be, the bound alone decides.
A program may use at most 128 MiB of HBM per device.

```python
import jax
import jax.numpy as jnp
from jax import lax

B = 64
CB = 64
KNZ = 15
AGG = 8
PNZ = 3
NB = 512


def draw_k_cols(key, part):
    reach = AGG
    span = 2 * reach - 2
    scores = jax.random.randint(key, (NB, span), 0, 1 << 20) * span + jnp.arange(span)[None, :]
    order = jnp.argsort(scores, axis=1)
    chosen = order[:, :KNZ - 3]
    candidates = jnp.concatenate([jnp.arange(-(reach - 1), 0), jnp.arange(1, reach)])
    offsets = candidates[chosen]
    fixed = jnp.broadcast_to(jnp.array([0, -reach, reach]), (NB, 3))
    block_rows = jnp.arange(NB)[:, None]
    return (block_rows + jnp.concatenate([fixed, offsets], axis=1)).astype(jnp.int32)


def draw_p_cols(key, part):
    first_key = jax.random.fold_in(key, 11)
    second_key = jax.random.fold_in(key, 23)
    scores = jax.random.randint(first_key, (NB, 3), 0, 1 << 20) * 3 + jnp.arange(3)[None, :]
    offsets = jnp.argsort(scores, axis=1) - 1
    keeper = jax.random.randint(second_key, (NB, 3), 0, 3) > 0
    keeper = keeper | (offsets == 0)
    aggregate = jnp.arange(NB)[:, None] // AGG
    columns = aggregate + offsets
    inside = (columns >= 0) & (columns < NB // AGG)
    return jnp.where(keeper & inside, columns, -1).astype(jnp.int32)


def shard_levels(own_key, shape, cuts, least, largest):
    def one(dim, blocks):
        draws = jax.random.uniform(jax.random.fold_in(jax.random.fold_in(own_key, 6), dim), (blocks,), jnp.float32, least / len(cuts), largest / len(cuts))
        return jnp.repeat(jnp.exp(draws), shape[dim] // blocks).reshape((-1,) + (1,) * (len(shape) - dim - 1))

    gain = one(*cuts[0])
    for cut in cuts[1:]:
        gain = gain * one(*cut)
    return gain


def bell_draw(rng, shape, scale, most, split=(), kind=jnp.bfloat16):
    values = jax.random.normal(rng, shape, jnp.float32) * scale
    if len(split) > 0:
        values = shard_levels(rng, shape, split, -0.22, 0.18) * values
    return jnp.clip(values, min=-most, max=most).astype(kind)


def setup_inputs(seed: int = 0) -> dict:
    key_of = jax.random.split(jax.random.key(seed), 5)
    return {
        "k_vals": bell_draw(key_of[0], (NB, KNZ, B, B), (B * KNZ) ** -0.5, 0.1875, ((0, 32),), jnp.float32),
        "k_cols": draw_k_cols(jax.random.fold_in(key_of[4], 71), 0),
        "p_vals": bell_draw(key_of[2], (NB, PNZ, B, CB), 0.2, 1.2, ((0, 32), (3, 16)), jnp.float32),
        "p_cols": draw_p_cols(jax.random.fold_in(key_of[4], 71), 0),
    }


def place_window(p_vals, p_cols, aggregate, blocks_all):
    present = (p_cols >= 0) & (p_cols < blocks_all)
    position = p_cols - aggregate[:, None] + 1
    selector = ((position[:, :, None] == jnp.arange(3, dtype=jnp.int32)[None, None, :]) & present[:, :, None]).astype(jnp.float32)
    return jnp.einsum("jtu,jtbc->jubc", selector, p_vals, precision=lax.Precision.HIGHEST)


def reference(k_vals, k_cols, p_vals, p_cols):
    total_rows = k_vals.shape[0]
    blocks_all = total_rows // AGG
    width = p_vals.shape[3]
    aggregate = jnp.arange(total_rows, dtype=jnp.int32) // AGG
    window = place_window(p_vals, p_cols, aggregate, blocks_all)
    in_range = (k_cols >= 0) & (k_cols < total_rows)
    safe_cols = jnp.clip(k_cols, 0, total_rows - 1).astype(jnp.int32)
    near_agg = safe_cols // AGG - aggregate[:, None] + 1
    side_mask = ((near_agg[:, :, None] == jnp.arange(3, dtype=jnp.int32)[None, None, :]) & in_range[:, :, None]).astype(jnp.float32)

    def one_row(triple):
        blocks, columns, masks = triple
        pieces = jnp.take(window, columns, axis=0)
        product = jnp.einsum("sab,subc->suac", blocks, pieces, precision=lax.Precision.HIGHEST)
        mixed_terms = jnp.einsum("se,suac->euac", masks, product, precision=lax.Precision.HIGHEST)
        result = jnp.zeros((5,) + mixed_terms.shape[2:], jnp.float32)
        for offset in range(3):
            result = result.at[offset:offset + 3].add(mixed_terms[offset])
        return result

    stiff_prolong = lax.map(one_row, (k_vals, safe_cols, side_mask))
    coarse = jnp.zeros((blocks_all, 7, width, width), jnp.float32)
    empty_row = jnp.zeros((1, width, width), jnp.float32)
    for left_slot in range(3):
        for right_slot in range(5):
            term = jnp.einsum("ibc,ibd->icd", window[:, left_slot], stiff_prolong[:, right_slot], precision=lax.Precision.HIGHEST)
            term = term.reshape(blocks_all, AGG, width, width).sum(axis=1)
            if left_slot == 0:
                moved = jnp.concatenate([term[1:], empty_row], axis=0)
            elif left_slot == 1:
                moved = term
            else:
                moved = jnp.concatenate([empty_row, term[:-1]], axis=0)
            coarse = coarse.at[:, right_slot - left_slot + 2].add(moved)
    return coarse
```

```python
import functools

import jax
import jax.numpy as jnp
from jax import lax
from jax.experimental import pallas as pl
from jax.experimental.pallas import tpu as pltpu
from jax.sharding import PartitionSpec as P

AGG = 8
RING = 8
MESH = pl.DeviceIdType.MESH
F32 = jnp.float32
BF16 = jnp.bfloat16


def kernel(
    row_count,
    p_cols,
    k_cols,
    p_hbm,
    k_hbm,
    out,
    p_buf,
    k_buf,
    k_split,
    chunk,
    ring,
    halo_out,
    halo_in,
    table,
    weights,
    left_side,
    terms,
    mine,
    side_out,
    side_in,
    final,
    p_sem,
    k_sem,
    ring_send,
    ring_recv,
    pair_sem,
    halo_send,
    halo_recv,
    side_send,
    side_recv,
):
    row = lax.axis_index("row")
    col = lax.axis_index("col")
    z = lax.div(col, 2)
    core = lax.rem(col, 2)
    right = (row, lax.rem(z + 1, RING) * 2 + core)
    left = (row, lax.rem(z + RING - 1, RING) * 2 + core)
    twin = (row, z * 2 + 1 - core)
    above = [(lax.rem(row + 1, row_count), z * 2 + n) for n in range(2)]
    below = [(lax.rem(row + row_count - 1, row_count), z * 2 + n) for n in range(2)]
    peers = [right, left, twin] + above + below

    barrier = pltpu.get_barrier_semaphore()
    for peer in peers:
        pl.semaphore_signal(barrier, inc=1, device_id=peer, device_id_type=MESH)
    p_copy = pltpu.make_async_copy(p_hbm, p_buf, p_sem)
    p_copy.start()
    k_copies = []
    for part in range(4):
        rows = pl.ds(4 * part, 4)
        k_copies.append(pltpu.make_async_copy(k_hbm.at[rows], k_buf.at[rows], k_sem.at[part]))
        k_copies[-1].start()

    own_rows = 2 * AGG
    first_row = row * own_rows
    total_rows = row_count * own_rows
    blocks_all = total_rows // AGG
    top = lax.broadcasted_iota(jnp.int32, (8, 128), 0) < 4
    low = lax.broadcasted_iota(jnp.int32, (8, 128), 1) < 64

    def swap_rows(value):
        return pltpu.roll(value, 4, 0)

    def swap_lanes(value):
        return pltpu.roll(value, 64, 1)

    p_copy.wait()

    def window(j, u):
        total = jnp.zeros((4, 64), F32)
        for t in range(3):
            block = p_cols[t, j]
            position = block - (2 * row + j // AGG) + 1
            position = jnp.where((block >= 0) & (block < blocks_all), position, -1)
            total = total + jnp.where(jnp.full((4, 64), position) == u, p_buf[j, t], 0.0)
        return total

    for m in range(4):
        for u in range(3):
            halves = [
                jnp.concatenate([window(g * AGG + 2 * m, u), window(g * AGG + 2 * m + 1, u)], axis=1)
                for g in range(2)
            ]
            chunk[core, m * 3 + u] = jnp.concatenate(halves, axis=0)
    for m in range(2):
        for u in range(3):
            even, odd = chunk[core, 2 * m * 3 + u], chunk[core, (2 * m + 1) * 3 + u]
            mixed = swap_rows(jnp.where(top, odd, even))
            halo_out[0, m * 3 + u] = jnp.where(top, even, mixed)
            halo_out[1, m * 3 + u] = jnp.where(top, mixed, odd)

    pl.semaphore_wait(barrier, len(peers))

    def ring_copy(way, step, half):
        part = pl.ds(6 * half, 6)
        slot = 7 - step if way == 0 else 1 + step
        before = slot + 1 if way == 0 else slot - 1
        source = chunk.at[core, part] if step == 0 else ring.at[before, part]
        return pltpu.make_async_remote_copy(
            src_ref=source,
            dst_ref=ring.at[slot, part],
            send_sem=ring_send.at[way, step, half],
            recv_sem=ring_recv.at[way, step, half],
            device_id=right if way == 0 else left,
            device_id_type=MESH,
        )

    started = []
    ring_copies = {}

    def send_ring(step, half):
        for way in range(2):
            if step < 3 or way == half:
                copy = ring_copy(way, step, half)
                copy.start()
                started.append(copy)
                ring_copies[way, step, half] = copy

    def take_ring(step, half):
        for way in range(2):
            if step < 3 or way == half:
                ring_copies[way, step, half].wait_recv()

    for half in range(2):
        send_ring(0, half)
    pair_copy = pltpu.make_async_remote_copy(
        src_ref=chunk.at[core],
        dst_ref=chunk.at[core],
        send_sem=pair_sem.at[0],
        recv_sem=pair_sem.at[1],
        device_id=twin,
        device_id_type=MESH,
    )
    pair_copy.start()

    def halo_copy(way, n, sender):
        return pltpu.make_async_remote_copy(
            src_ref=halo_out.at[way],
            dst_ref=halo_in.at[way, sender],
            send_sem=halo_send.at[way, n],
            recv_sem=halo_recv.at[way, sender],
            device_id=(below if way == 0 else above)[n],
            device_id_type=MESH,
        )

    for way in range(2):
        for n in range(2):
            copy = halo_copy(way, n, core)
            copy.start()
            started.append(copy)

    def split_k(i, carry):
        for q in range(4):
            pairs = []
            for s in (4 * q, 4 * q + 2):
                second = k_buf[i, s + 1] if s + 1 < 15 else jnp.zeros((64, 64), F32)
                pairs.append(jnp.concatenate([k_buf[i, s], second], axis=1))
            both = jnp.concatenate(pairs, axis=1)
            high = both.astype(BF16)
            k_split[i, q, 0:64] = high
            k_split[i, q, 64:128] = (both - high.astype(F32)).astype(BF16)
        return carry

    def split_part(part):
        k_copies[part].wait()
        lax.fori_loop(4 * part, 4 * part + 4, split_k, 0)

    split_part(0)
    split_part(1)
    take_ring(0, 0)
    send_ring(1, 0)
    take_ring(0, 1)
    send_ring(1, 1)
    split_part(2)
    split_part(3)

    def merge(zero, one):
        mixed = swap_rows(jnp.where(top, one, zero))
        return jnp.where(top, zero, mixed), jnp.where(top, mixed, one)

    def place(pair, side, tiles):
        for flipped in range(2):
            blocks = [swap_lanes(tile) for tile in tiles] if flipped else list(tiles)
            if side > 0:
                blocks = [jnp.zeros((8 * side, 128), F32)] + blocks
            if side < 3:
                blocks = blocks + [jnp.zeros((8 * (3 - side), 128), F32)]
            whole = jnp.concatenate(blocks, axis=0)
            high = whole.astype(BF16)
            table[2 * pair + flipped, 0] = high
            table[2 * pair + flipped, 1] = (whole - high.astype(F32)).astype(BF16)

    pair_copy.wait_recv()
    table[32:34] = jnp.zeros((2, 2, 48, 128), BF16)

    def place_own(m, carry):
        merged = [merge(chunk[0, m * 3 + u], chunk[1, m * 3 + u]) for u in range(3)]
        for g in range(2):
            place(4 + 4 * g + m, 1 + g, [merged[u][g] for u in range(3)])
        return carry

    lax.fori_loop(0, 4, place_own, 0)
    for way in range(2):
        for n in range(2):
            halo_copy(way, n, n).wait_recv()

    def place_halo(m, carry):
        for way, base, side in ((1, 0, 0), (0, 12, 3)):
            merged = [merge(halo_in[way, 0, m * 3 + u], halo_in[way, 1, m * 3 + u]) for u in range(3)]
            for x in range(2):
                place(base + 2 * m + x, side, [merged[u][x] for u in range(3)])
        return carry

    lax.fori_loop(0, 2, place_halo, 0)
    take_ring(1, 0)
    send_ring(2, 0)
    take_ring(1, 1)
    send_ring(2, 1)

    def entry(i, s):
        if s >= 15:
            return 32
        block = k_cols[i, s]
        near = block - first_row + AGG
        inside = (block >= 0) & (block < total_rows) & (near >= 0) & (near < 32)
        return jnp.where(inside, near, 32)

    low_16 = lax.broadcasted_iota(jnp.int32, (48, 128), 1) < 64
    blank = jnp.zeros((16, 128), BF16)

    def multiply_row(i, group):
        total = None
        for q in range(4):
            sides = []
            for s in (4 * q, 4 * q + 2):
                even = entry(i, s)
                odd = lax.bitwise_xor(entry(i, s + 1), 1)
                parts = [
                    jnp.where(low_16, table[even, part], table[odd, part]) for part in range(2)
                ]
                if group == 1:
                    parts = parts[::-1]
                sides.append(jnp.concatenate([parts[0], blank, parts[1], blank], axis=0))
            term = lax.dot_general(
                k_split[i, q],
                jnp.concatenate(sides, axis=1),
                (((1,), (1,)), ((), ())),
                preferred_element_type=F32,
            )
            total = term if total is None else total + term
        return total[0:64], total[64:128]

    low_64 = lax.broadcasted_iota(jnp.int32, (64, 128), 1) < 64

    def multiply(i, carry):
        a_0, b_0 = multiply_row(i, 0)
        a_1, b_1 = multiply_row(i + AGG, 1)
        value = jnp.where(low_64, a_0 + b_0, a_1 + b_1)
        value = value + swap_lanes(jnp.where(low_64, a_1, a_0))
        high = value.astype(BF16)
        rows = pl.ds(pl.multiple_of(64 * i, 64), 64)
        weights[rows, 0:128] = high
        weights[rows, 128:256] = (value - high.astype(F32)).astype(BF16)
        return carry

    lax.fori_loop(0, 4, multiply, 0)
    take_ring(2, 0)
    send_ring(3, 0)
    take_ring(2, 1)
    send_ring(3, 1)
    lax.fori_loop(4, 8, multiply, 0)

    order = (0, 1, 7, 2, 6, 3, 5, 4)

    def prepare(place_at, slot):
        def tile(m, u):
            return chunk[core, m * 3 + u] if slot == 0 else ring[slot, m * 3 + u]

        whole = jnp.concatenate(
            [jnp.concatenate([tile(m, u) for m in range(4)], axis=1) for u in range(3)], axis=0
        )
        rest = whole - whole.astype(BF16).astype(F32)
        left_side[pl.ds(48 * place_at, 48)] = jnp.concatenate([whole, rest], axis=0).astype(BF16)

    def products(first, count):
        result = lax.dot_general(
            left_side[pl.ds(48 * first, 48 * count)],
            weights[...],
            (((1,), (0,)), ((), ())),
            preferred_element_type=F32,
        )
        for n in range(count):
            base = 48 * n
            folded = []
            for u in range(3):
                a = base + 8 * u
                value = result[a : a + 8, 0:128] + result[a : a + 8, 128:256]
                value = value + result[a + 24 : a + 32, 0:128]
                folded.append(jnp.where(top, value, swap_lanes(value)))
            middle = folded[1] + swap_rows(jnp.where(top, folded[2], folded[0]))
            outer = jnp.where(top, folded[0], folded[2])
            slot = order[first + n]
            terms[0, slot] = jnp.where(top, pltpu.roll(middle, 8, 1), middle)
            terms[1, slot] = jnp.where(top, pltpu.roll(outer, 16, 1), pltpu.roll(outer, 120, 1))

    for n in range(5):
        prepare(n, order[n])
    products(0, 5)
    for n in range(5, 7):
        prepare(n, order[n])
    take_ring(3, 0)
    take_ring(3, 1)
    prepare(7, order[7])
    products(5, 3)

    def packed(kind, t):
        return jnp.where(low, terms[kind, t], swap_lanes(terms[kind, t + 4]))

    for t in range(4):
        mine[core, t] = packed(0, t)
    for t in range(2):
        one, two = packed(1, t), packed(1, t + 2)
        side_out[0, t] = jnp.where(top, one, swap_rows(two))
        side_out[1, t] = jnp.where(top, swap_rows(one), two)

    def side_copy(way, n, sender):
        return pltpu.make_async_remote_copy(
            src_ref=side_out.at[way],
            dst_ref=side_in.at[way, sender],
            send_sem=side_send.at[way, n],
            recv_sem=side_recv.at[way, sender],
            device_id=(below if way == 0 else above)[n],
            device_id_type=MESH,
        )

    for way in range(2):
        for n in range(2):
            copy = side_copy(way, n, core)
            copy.start()
            started.append(copy)
    twin_copy = pltpu.make_async_remote_copy(
        src_ref=mine.at[core],
        dst_ref=mine.at[core],
        send_sem=pair_sem.at[2],
        recv_sem=pair_sem.at[3],
        device_id=twin,
        device_id_type=MESH,
    )
    twin_copy.start()
    for copy in started:
        copy.wait_send()
    pair_copy.wait_send()
    twin_copy.wait()
    for way in range(2):
        for n in range(2):
            side_copy(way, n, n).wait_recv()

    for t in range(4):
        sums = []
        for n in range(2):
            up, down = side_in[1, n, t % 2], side_in[0, n, t % 2]
            if t < 2:
                other = jnp.where(top, up, swap_rows(down))
            else:
                other = jnp.where(top, swap_rows(up), down)
            sums.append(mine[n, t] + other)
        first = jnp.where(top, sums[0], swap_rows(sums[1]))
        second = jnp.where(top, swap_rows(sums[0]), sums[1])
        final[lax.rem(z + t, RING)] = jnp.where(low, first, swap_lanes(second))
        final[lax.rem(z + t + 4, RING)] = jnp.where(low, swap_lanes(first), second)
    turned = jnp.transpose(jnp.concatenate([final[n] for n in range(RING)], axis=0))
    even_core = jnp.full((4, 64), core) == 0
    for block in range(2):
        for band in range(7):
            a = 64 * block + 8 * band
            out[block, band] = jnp.where(even_core, turned[a : a + 4], turned[a + 4 : a + 8])


def body(row_count, k_vals, k_cols, p_vals, p_cols):
    own = k_vals.shape[0]
    dma = pltpu.SemaphoreType.DMA
    result = pl.pallas_call(
        functools.partial(kernel, row_count),
        out_shape=jax.ShapeDtypeStruct((2, 7, 4, 64), F32),
        in_specs=[
            pl.BlockSpec(memory_space=pltpu.SMEM),
            pl.BlockSpec(memory_space=pltpu.SMEM),
            pl.BlockSpec(memory_space=pl.ANY),
            pl.BlockSpec(memory_space=pl.ANY),
        ],
        out_specs=pl.BlockSpec(memory_space=pltpu.VMEM),
        scratch_shapes=[
            pltpu.VMEM((own, 3, 4, 64), F32),
            pltpu.VMEM((own, 15, 64, 64), F32),
            pltpu.VMEM((own, 4, 128, 256), BF16),
            pltpu.VMEM((2, 12, 8, 128), F32),
            pltpu.VMEM((RING, 12, 8, 128), F32),
            pltpu.VMEM((2, 6, 8, 128), F32),
            pltpu.VMEM((2, 2, 6, 8, 128), F32),
            pltpu.VMEM((34, 2, 48, 128), BF16),
            pltpu.VMEM((512, 256), BF16),
            pltpu.VMEM((384, 512), BF16),
            pltpu.VMEM((2, RING, 8, 128), F32),
            pltpu.VMEM((2, 4, 8, 128), F32),
            pltpu.VMEM((2, 2, 8, 128), F32),
            pltpu.VMEM((2, 2, 2, 8, 128), F32),
            pltpu.VMEM((RING, 8, 128), F32),
            dma,
            dma((4,)),
            dma((2, 4, 2)),
            dma((2, 4, 2)),
            dma((4,)),
            dma((2, 2)),
            dma((2, 2)),
            dma((2, 2)),
            dma((2, 2)),
        ],
        compiler_params=pltpu.CompilerParams(
            collective_id=0, has_side_effects=True, vmem_limit_bytes=40 * 1024 * 1024
        ),
    )(jnp.transpose(p_cols), k_cols, jnp.transpose(p_vals, (0, 1, 3, 2)), k_vals)
    return jnp.transpose(result, (0, 1, 3, 2))


def solution(mesh):
    placed = (
        P("row", None, None, None),
        P("row", None),
        P("row", None, None, "col"),
        P("row", None),
    )
    return jax.shard_map(
        functools.partial(body, mesh.shape["row"]),
        mesh=mesh,
        in_specs=placed,
        out_specs=P("row", None, None, "col"),
        check_vma=False,
    )
```

```python
import functools

import jax
import jax.numpy as jnp
from jax import lax
from jax.experimental import pallas as pl
from jax.experimental.pallas import tpu as pltpu
from jax.sharding import PartitionSpec as P

AGG = 8
RING = 8
PIECES = 2
REACH = (1, -1, 2, -2)
SENDS = 64
MESH = pl.DeviceIdType.MESH
F32 = jnp.float32
BF16 = jnp.bfloat16


def kernel(
    row_count,
    p_cols_hbm,
    k_cols_hbm,
    p_hbm,
    k_hbm,
    out,
    p_cols,
    k_cols,
    p_buf,
    k_buf,
    k_split,
    chunk,
    ring,
    halo_out,
    halo_in,
    table,
    weights,
    left_side,
    terms,
    mine,
    side_out,
    side_in,
    final,
    p_sem,
    cols_sem,
    k_sem,
    ring_send,
    ring_recv,
    pair_sem,
    halo_send,
    halo_recv,
    side_send,
    side_recv,
):
    row = lax.axis_index("row")
    col = lax.axis_index("col")
    z = lax.div(col, 2)
    core = lax.rem(col, 2)

    def along(places):
        return (row, lax.rem(z + places % RING, RING) * 2 + core)

    twin = (row, z * 2 + 1 - core)
    above = [(lax.rem(row + 1, row_count), z * 2 + n) for n in range(2)]
    below = [(lax.rem(row + row_count - 1, row_count), z * 2 + n) for n in range(2)]
    peers = [along(places) for places in REACH] + [twin] + above + below

    p_copy = pltpu.make_async_copy(p_hbm, p_buf, p_sem)
    p_copy.start()
    cols_copies = [
        pltpu.make_async_copy(p_cols_hbm, p_cols, cols_sem.at[0]),
        pltpu.make_async_copy(k_cols_hbm, k_cols, cols_sem.at[1]),
    ]
    for copy in cols_copies:
        copy.start()
    barrier = pltpu.get_barrier_semaphore()
    for peer in peers:
        pl.semaphore_signal(barrier, inc=1, device_id=peer, device_id_type=MESH)
    k_copies = []
    for part in range(4):
        rows = pl.ds(4 * part, 4)
        k_copies.append(pltpu.make_async_copy(k_hbm.at[rows], k_buf.at[rows], k_sem.at[part]))
        k_copies[-1].start()

    own_rows = 2 * AGG
    first_row = row * own_rows
    total_rows = row_count * own_rows
    blocks_all = total_rows // AGG
    top = lax.broadcasted_iota(jnp.int32, (8, 128), 0) < 4
    low = lax.broadcasted_iota(jnp.int32, (8, 128), 1) < 64

    def swap_rows(value):
        return pltpu.roll(value, 4, 0)

    def swap_lanes(value):
        return pltpu.roll(value, 64, 1)

    cols_copies[0].wait()
    p_copy.wait()

    def window(j, u):
        total = jnp.zeros((4, 64), F32)
        for t in range(3):
            block = p_cols[t, j]
            position = block - (2 * row + j // AGG) + 1
            position = jnp.where((block >= 0) & (block < blocks_all), position, -1)
            total = total + jnp.where(jnp.full((4, 64), position) == u, p_buf[j, t], 0.0)
        return total

    for m in range(4):
        for u in range(3):
            halves = [
                jnp.concatenate([window(g * AGG + 2 * m, u), window(g * AGG + 2 * m + 1, u)], axis=1)
                for g in range(2)
            ]
            chunk[core, m * 3 + u] = jnp.concatenate(halves, axis=0)
    for m in range(2):
        for u in range(3):
            even, odd = chunk[core, 2 * m * 3 + u], chunk[core, (2 * m + 1) * 3 + u]
            mixed = swap_rows(jnp.where(top, odd, even))
            halo_out[0, m * 3 + u] = jnp.where(top, even, mixed)
            halo_out[1, m * 3 + u] = jnp.where(top, mixed, odd)

    pl.semaphore_wait(barrier, len(peers))

    started = []
    width = 12 // PIECES

    def ring_copy(slot, places, piece, index):
        part = pl.ds(width * piece, width)
        source = chunk.at[core, part] if slot == 0 else ring.at[slot, part]
        target = (slot - places) % RING
        return pltpu.make_async_remote_copy(
            src_ref=source,
            dst_ref=ring.at[target, part],
            send_sem=ring_send.at[index],
            recv_sem=ring_recv.at[target, piece],
            device_id=along(places),
            device_id_type=MESH,
        )

    def send(slot, places, piece):
        copy = ring_copy(slot, places, piece, len(ring_started))
        copy.start()
        started.append(copy)
        ring_started.append(copy)

    ring_started = []

    def take(slot, piece):
        ring_copy((slot + 1) % RING, 1, piece, 0).wait_recv()

    for piece in range(PIECES):
        send(0, 2, piece)
        send(0, -2, piece)
    for piece in range(PIECES):
        send(0, 1, piece)
        send(0, -1, piece)
    pair_copy = pltpu.make_async_remote_copy(
        src_ref=chunk.at[core],
        dst_ref=chunk.at[core],
        send_sem=pair_sem.at[0],
        recv_sem=pair_sem.at[1],
        device_id=twin,
        device_id_type=MESH,
    )
    pair_copy.start()

    def halo_copy(way, n, sender):
        return pltpu.make_async_remote_copy(
            src_ref=halo_out.at[way],
            dst_ref=halo_in.at[way, sender],
            send_sem=halo_send.at[way, n],
            recv_sem=halo_recv.at[way, sender],
            device_id=(below if way == 0 else above)[n],
            device_id_type=MESH,
        )

    for way in range(2):
        for n in range(2):
            copy = halo_copy(way, n, core)
            copy.start()
            started.append(copy)

    def split_k(i, carry):
        for q in range(4):
            pairs = []
            for s in (4 * q, 4 * q + 2):
                second = k_buf[i, s + 1] if s + 1 < 15 else jnp.zeros((64, 64), F32)
                pairs.append(jnp.concatenate([k_buf[i, s], second], axis=1))
            both = jnp.concatenate(pairs, axis=1)
            high = both.astype(BF16)
            k_split[i, q, 0:64] = high
            k_split[i, q, 64:128] = (both - high.astype(F32)).astype(BF16)
        return carry

    def split_part(part):
        k_copies[part].wait()
        lax.fori_loop(4 * part, 4 * part + 4, split_k, 0)

    split_part(0)
    split_part(1)
    for piece in range(PIECES):
        take(6, piece)
        if piece < PIECES // 2:
            send(6, 2, piece)
        send(6, 1, piece)
        take(2, piece)
        if piece >= PIECES // 2:
            send(2, -2, piece)
        send(2, -1, piece)
    split_part(2)
    split_part(3)

    def merge(zero, one):
        mixed = swap_rows(jnp.where(top, one, zero))
        return jnp.where(top, zero, mixed), jnp.where(top, mixed, one)

    def place(pair, side, tiles):
        for flipped in range(2):
            blocks = [swap_lanes(tile) for tile in tiles] if flipped else list(tiles)
            if side > 0:
                blocks = [jnp.zeros((8 * side, 128), F32)] + blocks
            if side < 3:
                blocks = blocks + [jnp.zeros((8 * (3 - side), 128), F32)]
            whole = jnp.concatenate(blocks, axis=0)
            high = whole.astype(BF16)
            table[2 * pair + flipped, 0] = high
            table[2 * pair + flipped, 1] = (whole - high.astype(F32)).astype(BF16)

    pair_copy.wait_recv()
    table[32:34] = jnp.zeros((2, 2, 48, 128), BF16)

    def place_own(m, carry):
        merged = [merge(chunk[0, m * 3 + u], chunk[1, m * 3 + u]) for u in range(3)]
        for g in range(2):
            place(4 + 4 * g + m, 1 + g, [merged[u][g] for u in range(3)])
        return carry

    lax.fori_loop(0, 4, place_own, 0)
    for way in range(2):
        for n in range(2):
            halo_copy(way, n, n).wait_recv()

    def place_halo(m, carry):
        for way, base, side in ((1, 0, 0), (0, 12, 3)):
            merged = [merge(halo_in[way, 0, m * 3 + u], halo_in[way, 1, m * 3 + u]) for u in range(3)]
            for x in range(2):
                place(base + 2 * m + x, side, [merged[u][x] for u in range(3)])
        return carry

    lax.fori_loop(0, 2, place_halo, 0)
    pass

    cols_copies[1].wait()

    def entry(i, s):
        if s >= 15:
            return 32
        block = k_cols[i, s]
        near = block - first_row + AGG
        inside = (block >= 0) & (block < total_rows) & (near >= 0) & (near < 32)
        return jnp.where(inside, near, 32)

    low_16 = lax.broadcasted_iota(jnp.int32, (48, 128), 1) < 64
    blank = jnp.zeros((16, 128), BF16)

    def multiply_row(i, group):
        total = None
        for q in range(4):
            sides = []
            for s in (4 * q, 4 * q + 2):
                even = entry(i, s)
                odd = lax.bitwise_xor(entry(i, s + 1), 1)
                parts = [
                    jnp.where(low_16, table[even, part], table[odd, part]) for part in range(2)
                ]
                if group == 1:
                    parts = parts[::-1]
                sides.append(jnp.concatenate([parts[0], blank, parts[1], blank], axis=0))
            term = lax.dot_general(
                k_split[i, q],
                jnp.concatenate(sides, axis=1),
                (((1,), (1,)), ((), ())),
                preferred_element_type=F32,
            )
            total = term if total is None else total + term
        return total[0:64], total[64:128]

    low_64 = lax.broadcasted_iota(jnp.int32, (64, 128), 1) < 64

    def multiply(i, carry):
        a_0, b_0 = multiply_row(i, 0)
        a_1, b_1 = multiply_row(i + AGG, 1)
        value = jnp.where(low_64, a_0 + b_0, a_1 + b_1)
        value = value + swap_lanes(jnp.where(low_64, a_1, a_0))
        high = value.astype(BF16)
        rows = pl.ds(pl.multiple_of(64 * i, 64), 64)
        weights[rows, 0:128] = high
        weights[rows, 128:256] = (value - high.astype(F32)).astype(BF16)
        return carry

    lax.fori_loop(0, 4, multiply, 0)
    for piece in range(PIECES):
        take(7, piece)
        take(1, piece)
    lax.fori_loop(4, 8, multiply, 0)

    order = (0, 1, 7, 2, 6, 3, 5, 4)

    def prepare(place_at, slot):
        def tile(m, u):
            return chunk[core, m * 3 + u] if slot == 0 else ring[slot, m * 3 + u]

        whole = jnp.concatenate(
            [jnp.concatenate([tile(m, u) for m in range(4)], axis=1) for u in range(3)], axis=0
        )
        rest = whole - whole.astype(BF16).astype(F32)
        left_side[pl.ds(48 * place_at, 48)] = jnp.concatenate([whole, rest], axis=0).astype(BF16)

    def products(first, count):
        result = lax.dot_general(
            left_side[pl.ds(48 * first, 48 * count)],
            weights[...],
            (((1,), (0,)), ((), ())),
            preferred_element_type=F32,
        )
        for n in range(count):
            base = 48 * n
            folded = []
            for u in range(3):
                a = base + 8 * u
                value = result[a : a + 8, 0:128] + result[a : a + 8, 128:256]
                value = value + result[a + 24 : a + 32, 0:128]
                folded.append(jnp.where(top, value, swap_lanes(value)))
            middle = folded[1] + swap_rows(jnp.where(top, folded[2], folded[0]))
            outer = jnp.where(top, folded[0], folded[2])
            slot = order[first + n]
            terms[0, slot] = jnp.where(top, pltpu.roll(middle, 8, 1), middle)
            terms[1, slot] = jnp.where(top, pltpu.roll(outer, 16, 1), pltpu.roll(outer, 120, 1))

    for n in range(5):
        prepare(n, order[n])
    products(0, 5)
    for piece in range(PIECES):
        for slot in (3, 5, 4):
            take(slot, piece)
    for n in range(5, 8):
        prepare(n, order[n])
    products(5, 3)

    def packed(kind, t):
        return jnp.where(low, terms[kind, t], swap_lanes(terms[kind, t + 4]))

    for t in range(4):
        mine[core, t] = packed(0, t)
    for t in range(2):
        one, two = packed(1, t), packed(1, t + 2)
        side_out[0, t] = jnp.where(top, one, swap_rows(two))
        side_out[1, t] = jnp.where(top, swap_rows(one), two)

    def side_copy(way, n, sender):
        return pltpu.make_async_remote_copy(
            src_ref=side_out.at[way],
            dst_ref=side_in.at[way, sender],
            send_sem=side_send.at[way, n],
            recv_sem=side_recv.at[way, sender],
            device_id=(below if way == 0 else above)[n],
            device_id_type=MESH,
        )

    for way in range(2):
        for n in range(2):
            copy = side_copy(way, n, core)
            copy.start()
            started.append(copy)
    twin_copy = pltpu.make_async_remote_copy(
        src_ref=mine.at[core],
        dst_ref=mine.at[core],
        send_sem=pair_sem.at[2],
        recv_sem=pair_sem.at[3],
        device_id=twin,
        device_id_type=MESH,
    )
    twin_copy.start()
    twin_copy.wait_recv()
    for way in range(2):
        for n in range(2):
            side_copy(way, n, n).wait_recv()

    for t in range(4):
        sums = []
        for n in range(2):
            up, down = side_in[1, n, t % 2], side_in[0, n, t % 2]
            if t < 2:
                other = jnp.where(top, up, swap_rows(down))
            else:
                other = jnp.where(top, swap_rows(up), down)
            sums.append(mine[n, t] + other)
        first = jnp.where(top, sums[0], swap_rows(sums[1]))
        second = jnp.where(top, swap_rows(sums[0]), sums[1])
        final[lax.rem(z + t, RING)] = jnp.where(low, first, swap_lanes(second))
        final[lax.rem(z + t + 4, RING)] = jnp.where(low, swap_lanes(first), second)
    turned = jnp.transpose(jnp.concatenate([final[n] for n in range(RING)], axis=0))
    even_core = jnp.full((4, 64), core) == 0
    for block in range(2):
        for band in range(7):
            a = 64 * block + 8 * band
            out[block, band] = jnp.where(even_core, turned[a : a + 4], turned[a + 4 : a + 8])
    for copy in started + [pair_copy, twin_copy]:
        copy.wait_send()


def body(row_count, k_vals, k_cols, p_vals, p_cols):
    own = k_vals.shape[0]
    dma = pltpu.SemaphoreType.DMA
    result = pl.pallas_call(
        functools.partial(kernel, row_count),
        out_shape=jax.ShapeDtypeStruct((2, 7, 4, 64), F32),
        in_specs=[
            pl.BlockSpec(memory_space=pl.ANY),
            pl.BlockSpec(memory_space=pl.ANY),
            pl.BlockSpec(memory_space=pl.ANY),
            pl.BlockSpec(memory_space=pl.ANY),
        ],
        out_specs=pl.BlockSpec(memory_space=pltpu.VMEM),
        scratch_shapes=[
            pltpu.SMEM((3, own), jnp.int32),
            pltpu.SMEM((own, 15), jnp.int32),
            pltpu.VMEM((own, 3, 4, 64), F32),
            pltpu.VMEM((own, 15, 64, 64), F32),
            pltpu.VMEM((own, 4, 128, 256), BF16),
            pltpu.VMEM((2, 12, 8, 128), F32),
            pltpu.VMEM((RING, 12, 8, 128), F32),
            pltpu.VMEM((2, 6, 8, 128), F32),
            pltpu.VMEM((2, 2, 6, 8, 128), F32),
            pltpu.VMEM((34, 2, 48, 128), BF16),
            pltpu.VMEM((512, 256), BF16),
            pltpu.VMEM((384, 512), BF16),
            pltpu.VMEM((2, RING, 8, 128), F32),
            pltpu.VMEM((2, 4, 8, 128), F32),
            pltpu.VMEM((2, 2, 8, 128), F32),
            pltpu.VMEM((2, 2, 2, 8, 128), F32),
            pltpu.VMEM((RING, 8, 128), F32),
            dma,
            dma((2,)),
            dma((4,)),
            dma((SENDS,)),
            dma((RING, PIECES)),
            dma((4,)),
            dma((2, 2)),
            dma((2, 2)),
            dma((2, 2)),
            dma((2, 2)),
        ],
        compiler_params=pltpu.CompilerParams(
            collective_id=0, has_side_effects=True, vmem_limit_bytes=62 * 1024 * 1024
        ),
    )(jnp.transpose(p_cols), k_cols, jnp.transpose(p_vals, (0, 1, 3, 2)), k_vals)
    return jnp.transpose(result, (0, 1, 3, 2))


def solution(mesh):
    placed = (
        P("row", None, None, None),
        P("row", None),
        P("row", None, None, "col"),
        P("row", None),
    )
    return jax.shard_map(
        functools.partial(body, mesh.shape["row"]),
        mesh=mesh,
        in_specs=placed,
        out_specs=P("row", None, None, "col"),
        check_vma=False,
    )
```

```python
import functools

import jax
import jax.numpy as jnp
from jax import lax
from jax.experimental import pallas as pl
from jax.experimental.pallas import tpu as pltpu
from jax.sharding import PartitionSpec as P

AGG = 8
RING = 8
REACH = (2, -2, 1, -1)
MESH = pl.DeviceIdType.MESH
F32 = jnp.float32
BF16 = jnp.bfloat16


def kernel(
    row_count,
    p_cols_hbm,
    k_cols_hbm,
    p_hbm,
    k_hbm,
    out,
    p_cols,
    k_cols,
    p_buf,
    k_buf,
    k_split,
    near,
    ring,
    table,
    weights,
    left_side,
    terms,
    packed,
    twin_in,
    side_in,
    final,
    local_sem,
    ring_send,
    ring_recv,
    pair_sem,
    halo_send,
    halo_recv,
    side_send,
    side_recv,
):
    row = lax.axis_index("row")
    col = lax.axis_index("col")
    z = lax.div(col, 2)
    core = lax.rem(col, 2)
    own_rows = 2 * AGG
    first_row = row * own_rows
    total_rows = row_count * own_rows
    blocks_all = total_rows // AGG
    has_above = row < row_count - 1
    has_below = row > 0
    lower = core == 0
    has_side = jnp.where(lower, row, row_count - 1 - row) > 0
    has_other = jnp.where(lower, row_count - 1 - row, row) > 0
    side_row = row - 1 + 2 * core
    other_row = row + 1 - 2 * core
    twin = (row, z * 2 + 1 - core)

    def along(places, which):
        return (row, lax.rem(z + places % RING, RING) * 2 + which)

    copies = [
        pltpu.make_async_copy(p_hbm, p_buf, local_sem.at[0]),
        pltpu.make_async_copy(p_cols_hbm, p_cols, local_sem.at[1]),
        pltpu.make_async_copy(k_cols_hbm, k_cols, local_sem.at[2]),
    ]
    for copy in copies:
        copy.start()
    barrier = pltpu.get_barrier_semaphore()

    def greet(peer):
        pl.semaphore_signal(barrier, inc=1, device_id=peer, device_id_type=MESH)

    greet(twin)
    for places in REACH:
        for which in range(2):
            greet(along(places, which))

    @pl.when(has_side)
    def _():
        for which in range(2):
            greet((side_row, z * 2 + which))

    @pl.when(has_other)
    def _():
        greet((other_row, z * 2 + core))

    k_copies = []
    for part in range(2):
        k_copies.append(
            pltpu.make_async_copy(
                k_hbm.at[pl.ds(AGG * core + 4 * part, 4)], k_buf.at[pl.ds(4 * part, 4)], local_sem.at[3 + part]
            )
        )
        k_copies[-1].start()

    top = lax.broadcasted_iota(jnp.int32, (8, 128), 0) < 4
    low = lax.broadcasted_iota(jnp.int32, (8, 128), 1) < 64

    def swap_rows(value):
        return pltpu.roll(value, 4, 0)

    def swap_lanes(value):
        return pltpu.roll(value, 64, 1)

    copies[1].wait()
    copies[0].wait()

    def window(j, u):
        total = jnp.zeros((4, 64), F32)
        for t in range(3):
            block = p_cols[t, j]
            position = block - (2 * row + j // AGG) + 1
            position = jnp.where((block >= 0) & (block < blocks_all), position, -1)
            total = total + jnp.where(jnp.full((4, 64), position) == u, p_buf[j, t], 0.0)
        return total

    for h in range(2):
        for m in range(2):
            for u in range(3):
                halves = []
                for x in range(2):
                    j = AGG * h + 4 * m + 2 * x
                    halves.append(jnp.concatenate([window(j, u), window(j + 1, u)], axis=1))
                near[h + 1 - core, core, m * 3 + u] = jnp.concatenate(halves, axis=0)

    @pl.when(jnp.logical_not(has_side))
    def _():
        near[2 * core] = jnp.zeros((2, 6, 8, 128), F32)

    @pl.when(jnp.logical_not(has_below))
    def _():
        side_in[0] = jnp.zeros((4, 8, 128), F32)

    @pl.when(jnp.logical_not(has_above))
    def _():
        side_in[1] = jnp.zeros((4, 8, 128), F32)

    greeted = jnp.where(has_side, 2, 0) + jnp.where(has_other, 1, 0) + 2 * len(REACH) + 1
    pl.semaphore_wait(barrier, greeted)

    started = []

    def ring_copy(source, slot, places, which, part, index):
        target = (slot - places) % RING
        return pltpu.make_async_remote_copy(
            src_ref=source,
            dst_ref=ring.at[target, part],
            send_sem=ring_send.at[index],
            recv_sem=ring_recv.at[target, part],
            device_id=along(places, which),
            device_id_type=MESH,
        )

    def begin(*arguments):
        copy = ring_copy(*arguments, len(started))
        copy.start()
        started.append(copy)

    def take(slot, part):
        ring_copy(ring.at[slot, part], (slot + 1) % RING, 1, core, part, 0).wait_recv()

    for places in REACH:
        for h in range(2):
            begin(near.at[h + 1 - core, core], 0, places, h, core)

    pair_copy = pltpu.make_async_remote_copy(
        src_ref=near.at[pl.ds(1 - core, 2), core],
        dst_ref=near.at[pl.ds(core, 2), core],
        send_sem=pair_sem.at[0],
        recv_sem=pair_sem.at[1],
        device_id=twin,
        device_id_type=MESH,
    )
    pair_copy.start()
    pair_take = pltpu.make_async_remote_copy(
        src_ref=near.at[pl.ds(core, 2), 1 - core],
        dst_ref=near.at[pl.ds(1 - core, 2), 1 - core],
        send_sem=pair_sem.at[0],
        recv_sem=pair_sem.at[1],
        device_id=twin,
        device_id_type=MESH,
    )

    def halo_copy(h):
        return pltpu.make_async_remote_copy(
            src_ref=near.at[h + 1 - core, core],
            dst_ref=near.at[2 - 2 * h, core],
            send_sem=halo_send.at[h],
            recv_sem=halo_recv.at[core],
            device_id=(row - 1 + 2 * h, z * 2 + 1 - h),
            device_id_type=MESH,
        )

    def halo_take(sender):
        pltpu.make_async_remote_copy(
            src_ref=near.at[1, sender],
            dst_ref=near.at[2 * core, sender],
            send_sem=halo_send.at[0],
            recv_sem=halo_recv.at[sender],
            device_id=(side_row, z * 2 + sender),
            device_id_type=MESH,
        ).wait_recv()

    @pl.when(has_below)
    def _():
        halo_copy(0).start()

    @pl.when(has_above)
    def _():
        halo_copy(1).start()

    def split_k(i, carry):
        for q in range(4):
            pairs = []
            for s in (4 * q, 4 * q + 2):
                second = k_buf[i, s + 1] if s + 1 < 15 else jnp.zeros((64, 64), F32)
                pairs.append(jnp.concatenate([k_buf[i, s], second], axis=1))
            both = jnp.concatenate(pairs, axis=1)
            high = both.astype(BF16)
            k_split[i, q, 0:64] = high
            k_split[i, q, 64:128] = (both - high.astype(F32)).astype(BF16)
        return carry

    def split_part(part):
        k_copies[part].wait()
        lax.fori_loop(4 * part, 4 * part + 4, split_k, 0)

    def merge(zero, one):
        mixed = swap_rows(jnp.where(top, one, zero))
        return jnp.where(top, zero, mixed), jnp.where(top, mixed, one)

    def place_group(side):
        def place(m, carry):
            merged = [merge(near[side, 0, m * 3 + u], near[side, 1, m * 3 + u]) for u in range(3)]
            for x in range(2):
                for flipped in range(2):
                    blocks = [swap_lanes(merged[u][x]) if flipped else merged[u][x] for u in range(3)]
                    if side > 0:
                        blocks = [jnp.zeros((8 * side, 128), F32)] + blocks
                    whole = jnp.concatenate(blocks + [jnp.zeros((8 * (3 - side), 128), F32)], axis=0)
                    high = whole.astype(BF16)
                    entry_at = 8 * side + 4 * m + 2 * x + flipped
                    table[entry_at, 0] = high
                    table[entry_at, 1] = (whole - high.astype(F32)).astype(BF16)
            return carry

        lax.fori_loop(0, 2, place, 0)

    split_part(0)
    split_part(1)
    pair_take.wait_recv()
    table[24:26] = jnp.zeros((2, 2, 48, 128), BF16)
    place_group(1)
    for part in range(2):
        take(6, part)
        begin(ring.at[6, part], 6, 1, core, part)
        if part == 0:
            begin(ring.at[6, part], 6, 2, core, part)
        take(2, part)
        begin(ring.at[2, part], 2, -1, core, part)
        if part == 1:
            begin(ring.at[2, part], 2, -2, core, part)

    @pl.when(has_side)
    def _():
        for sender in range(2):
            halo_take(sender)

    place_group(0)
    place_group(2)
    copies[2].wait()

    def entry(i, s):
        if s >= 15:
            return 24
        block = k_cols[AGG * core + i, s]
        place_of = block - (first_row + AGG * core - AGG)
        inside = (block >= 0) & (block < total_rows) & (place_of >= 0) & (place_of < 24)
        return jnp.where(inside, place_of, 24)

    low_16 = lax.broadcasted_iota(jnp.int32, (48, 128), 1) < 64
    low_64 = lax.broadcasted_iota(jnp.int32, (64, 128), 1) < 64
    blank = jnp.zeros((16, 128), BF16)

    def multiply_row(i, swapped):
        total = None
        for q in range(4):
            sides = []
            for s in (4 * q, 4 * q + 2):
                even = entry(i, s)
                odd = lax.bitwise_xor(entry(i, s + 1), 1)
                parts = [jnp.where(low_16, table[even, part], table[odd, part]) for part in range(2)]
                if swapped:
                    parts = parts[::-1]
                sides.append(jnp.concatenate([parts[0], blank, parts[1], blank], axis=0))
            term = lax.dot_general(
                k_split[i, q],
                jnp.concatenate(sides, axis=1),
                (((1,), (1,)), ((), ())),
                preferred_element_type=F32,
            )
            total = term if total is None else total + term
        return total[0:64], total[64:128]

    def multiply(n, carry):
        i = n + 2 * (n // 2)
        a_0, b_0 = multiply_row(i, False)
        a_1, b_1 = multiply_row(i + 2, True)
        value = jnp.where(low_64, a_0 + b_0, a_1 + b_1)
        value = value + swap_lanes(jnp.where(low_64, a_1, a_0))
        high = value.astype(BF16)
        rows = pl.ds(pl.multiple_of(64 * n, 64), 64)
        weights[rows, 0:128] = high
        weights[rows, 128:256] = (value - high.astype(F32)).astype(BF16)
        return carry

    lax.fori_loop(0, 4, multiply, 0)

    def prepare(place_at, slot):
        for part in range(2):

            def tile(m, u):
                return near[1, part, m * 3 + u] if slot == 0 else ring[slot, part, m * 3 + u]

            whole = jnp.concatenate(
                [jnp.concatenate([tile(m, u) for m in range(2)], axis=1) for u in range(3)], axis=0
            )
            rest = whole - whole.astype(BF16).astype(F32)
            rows = pl.ds(96 * place_at + 48 * part, 48)
            left_side[rows] = jnp.concatenate([whole, rest], axis=0).astype(BF16)

    def products(first, slots):
        count = len(slots)
        result = lax.dot_general(
            left_side[pl.ds(96 * first, 96 * count)],
            weights[...],
            (((1,), (0,)), ((), ())),
            preferred_element_type=F32,
        )
        for n, slot in enumerate(slots):
            for u in range(3):
                folded = []
                for part in range(2):
                    a = 96 * n + 48 * part + 8 * u
                    value = result[a : a + 8, 0:128] + result[a : a + 8, 128:256]
                    value = value + result[a + 24 : a + 32, 0:128]
                    folded.append(jnp.where(top, value, swap_lanes(value)))
                value = jnp.where(top, folded[0], folded[1])
                value = value + swap_rows(jnp.where(top, folded[1], folded[0]))
                terms[u, slot] = value if u == 2 else pltpu.roll(value, 16 - 8 * u, 1)

    early, late = (0, 2, 6, 1, 7), (3, 5, 4)
    for part in range(2):
        take(7, part)
        take(1, part)
    for n, slot in enumerate(early):
        prepare(n, slot)
    products(0, early)
    for n, slot in enumerate(late):
        for part in range(2):
            take(slot, part)
        prepare(5 + n, slot)
    products(5, late)

    for u in range(3):
        for t in range(4):
            packed[u, t] = jnp.where(low, terms[u, t], swap_lanes(terms[u, t + 4]))

    def side_copy(n):
        return pltpu.make_async_remote_copy(
            src_ref=packed.at[2 * core],
            dst_ref=side_in.at[1 - core],
            send_sem=side_send.at[n],
            recv_sem=side_recv.at[1 - core],
            device_id=(side_row, z * 2 + n),
            device_id_type=MESH,
        )

    def side_take(n):
        pltpu.make_async_remote_copy(
            src_ref=packed.at[0],
            dst_ref=side_in.at[n],
            send_sem=side_send.at[0],
            recv_sem=side_recv.at[n],
            device_id=(row - 1 + 2 * n, z * 2 + 1 - n),
            device_id_type=MESH,
        ).wait_recv()

    @pl.when(has_side)
    def _():
        for n in range(2):
            side_copy(n).start()

    twin_copy = pltpu.make_async_remote_copy(
        src_ref=packed.at[pl.ds(1 - core, 2)],
        dst_ref=twin_in,
        send_sem=pair_sem.at[2],
        recv_sem=pair_sem.at[3],
        device_id=twin,
        device_id_type=MESH,
    )
    twin_copy.start()
    twin_copy.wait_recv()

    @pl.when(has_below)
    def _():
        side_take(0)

    @pl.when(has_above)
    def _():
        side_take(1)

    for t in range(4):
        first, second = [packed[n + 1 - core, t] + twin_in[n, t] + side_in[n, t] for n in range(2)]
        final[lax.rem(z + t, RING)] = jnp.where(low, first, swap_lanes(second))
        final[lax.rem(z + t + 4, RING)] = jnp.where(low, swap_lanes(first), second)
    turned = jnp.transpose(jnp.concatenate([final[n] for n in range(RING)], axis=0))
    even_core = jnp.full((4, 64), core) == 0
    for block in range(2):
        for band in range(7):
            a = 64 * block + 8 * band
            out[block, band] = jnp.where(even_core, turned[a : a + 4], turned[a + 4 : a + 8])

    for copy in started + [pair_copy, twin_copy]:
        copy.wait_send()

    @pl.when(has_below)
    def _():
        halo_copy(0).wait_send()

    @pl.when(has_above)
    def _():
        halo_copy(1).wait_send()

    @pl.when(has_side)
    def _():
        for n in range(2):
            side_copy(n).wait_send()


def body(row_count, k_vals, k_cols, p_vals, p_cols):
    own = k_vals.shape[0]
    dma = pltpu.SemaphoreType.DMA
    operands = [jnp.transpose(p_cols), k_cols, jnp.transpose(p_vals, (0, 1, 3, 2)), k_vals]
    result = pl.pallas_call(
        functools.partial(kernel, row_count),
        out_shape=jax.ShapeDtypeStruct((2, 7, 4, 64), F32),
        in_specs=[pl.BlockSpec(memory_space=pltpu.HBM)] * 4,
        out_specs=pl.BlockSpec(memory_space=pltpu.VMEM),
        scratch_shapes=[
            pltpu.SMEM((3, own), jnp.int32),
            pltpu.SMEM((own, 15), jnp.int32),
            pltpu.VMEM((own, 3, 4, 64), F32),
            pltpu.VMEM((AGG, 15, 64, 64), F32),
            pltpu.VMEM((AGG, 4, 128, 256), BF16),
            pltpu.VMEM((3, 2, 6, 8, 128), F32),
            pltpu.VMEM((RING, 2, 6, 8, 128), F32),
            pltpu.VMEM((26, 2, 48, 128), BF16),
            pltpu.VMEM((256, 256), BF16),
            pltpu.VMEM((768, 256), BF16),
            pltpu.VMEM((3, RING, 8, 128), F32),
            pltpu.VMEM((3, 4, 8, 128), F32),
            pltpu.VMEM((2, 4, 8, 128), F32),
            pltpu.VMEM((2, 4, 8, 128), F32),
            pltpu.VMEM((RING, 8, 128), F32),
            dma((5,)),
            dma((16,)),
            dma((RING, 2)),
            dma((4,)),
            dma((2,)),
            dma((2,)),
            dma((2,)),
            dma((2,)),
        ],
        compiler_params=pltpu.CompilerParams(
            collective_id=0, has_side_effects=True, vmem_limit_bytes=32 * 1024 * 1024
        ),
    )(*[pltpu.with_memory_space_constraint(operand, pltpu.HBM) for operand in operands])
    return jnp.transpose(result, (0, 1, 3, 2))


def solution(mesh):
    placed = (
        P("row", None, None, None),
        P("row", None),
        P("row", None, None, "col"),
        P("row", None),
    )
    return jax.shard_map(
        functools.partial(body, mesh.shape["row"]),
        mesh=mesh,
        in_specs=placed,
        out_specs=P("row", None, None, "col"),
        check_vma=False,
    )
```

```python
import functools

import jax
import jax.numpy as jnp
from jax import lax
from jax.experimental import pallas as pl
from jax.experimental.pallas import tpu as pltpu
from jax.sharding import PartitionSpec as P

AGG = 8
RING = 8
SPREAD = ((3, -3), (2, 2), (1, -1))
MESH = pl.DeviceIdType.MESH
F32 = jnp.float32
BF16 = jnp.bfloat16


def kernel(
    row_count,
    p_cols_hbm,
    k_cols_hbm,
    p_hbm,
    k_hbm,
    out,
    p_cols,
    k_cols,
    p_buf,
    k_buf,
    k_split,
    near,
    ring,
    table,
    weights,
    left_side,
    terms,
    packed,
    pair_in,
    side_in,
    final,
    local_sem,
    ring_send,
    ring_recv,
    pair_send,
    pair_recv,
    last_recv,
    halo_send,
    halo_recv,
    side_send,
    side_recv,
):
    row = lax.axis_index("row")
    col = lax.axis_index("col")
    z = lax.div(col, 2)
    core = lax.rem(col, 2)
    own_rows = 2 * AGG
    first_row = row * own_rows
    total_rows = row_count * own_rows
    blocks_all = total_rows // AGG
    has_above = row < row_count - 1
    has_below = row > 0
    lower = core == 0
    has_side = jnp.where(lower, row, row_count - 1 - row) > 0
    has_other = jnp.where(lower, row_count - 1 - row, row) > 0
    side_row = row - 1 + 2 * core
    other_row = row + 1 - 2 * core
    odd = lax.rem(z, 2)
    turn = 1 - 2 * odd
    me = odd * 2 + core

    def along(places, which):
        return (row, lax.rem(z + turn * places + RING, RING) * 2 + which)

    def member(at_row, number):
        return (at_row, (z - odd) * 2 + number)

    pair_peers = [(row, z * 2 + 1 - core), along(1, 0), along(1, 1)]

    copies = [
        pltpu.make_async_copy(p_hbm, p_buf, local_sem.at[0]),
        pltpu.make_async_copy(p_cols_hbm, p_cols, local_sem.at[1]),
        pltpu.make_async_copy(k_cols_hbm, k_cols, local_sem.at[2]),
    ]
    for copy in copies:
        copy.start()
    barrier = pltpu.get_barrier_semaphore()

    def greet(peer):
        pl.semaphore_signal(barrier, inc=1, device_id=peer, device_id_type=MESH)

    for peer in pair_peers:
        greet(peer)
    for places in (-1, 2, -2, -3):
        for which in range(2):
            greet(along(places, which))

    @pl.when(has_side)
    def _():
        for number in range(4):
            greet(member(side_row, number))

    @pl.when(has_other)
    def _():
        for n in range(2):
            greet(member(other_row, 2 * n + core))

    k_copies = []
    for part in range(2):
        k_copies.append(
            pltpu.make_async_copy(
                k_hbm.at[pl.ds(AGG * core + 4 * part, 4)], k_buf.at[pl.ds(4 * part, 4)], local_sem.at[3 + part]
            )
        )
        k_copies[-1].start()

    top = lax.broadcasted_iota(jnp.int32, (8, 128), 0) < 4
    low = lax.broadcasted_iota(jnp.int32, (8, 128), 1) < 64

    def swap_rows(value):
        return pltpu.roll(value, 4, 0)

    def swap_lanes(value):
        return pltpu.roll(value, 64, 1)

    copies[1].wait()
    copies[0].wait()

    def window(j, u):
        total = jnp.zeros((4, 64), F32)
        for t in range(3):
            block = p_cols[t, j]
            position = block - (2 * row + j // AGG) + 1
            position = jnp.where((block >= 0) & (block < blocks_all), position, -1)
            total = total + jnp.where(jnp.full((4, 64), position) == u, p_buf[j, t], 0.0)
        return total

    for h in range(2):
        for m in range(2):
            for u in range(3):
                halves = []
                for x in range(2):
                    j = AGG * h + 4 * m + 2 * x
                    halves.append(jnp.concatenate([window(j, u), window(j + 1, u)], axis=1))
                near[h + 1 - core, me, m * 3 + u] = jnp.concatenate(halves, axis=0)

    @pl.when(jnp.logical_not(has_side))
    def _():
        near[2 * core] = jnp.zeros((4, 6, 8, 128), F32)

    @pl.when(jnp.logical_not(has_below))
    def _():
        for n in range(2):
            side_in[n, 0] = jnp.zeros((8, 128), F32)

    @pl.when(jnp.logical_not(has_above))
    def _():
        for n in range(2):
            side_in[n, 1] = jnp.zeros((8, 128), F32)

    pl.semaphore_wait(barrier, jnp.where(has_side, 4, 0) + jnp.where(has_other, 2, 0) + 11)

    def pair_copy(n, number, which, peer):
        return pltpu.make_async_remote_copy(
            src_ref=near.at[pl.ds(1 - core, 2), number],
            dst_ref=near.at[pl.ds(1 - which, 2), number],
            send_sem=pair_send.at[n],
            recv_sem=pair_recv.at[number],
            device_id=peer,
            device_id_type=MESH,
        )

    started = []
    for n, peer in enumerate(pair_peers):
        started.append(pair_copy(n, me, 1 - core if n == 0 else n - 1, peer))
        started[-1].start()

    def halo_copy(h, n):
        return pltpu.make_async_remote_copy(
            src_ref=near.at[h + 1 - core, me],
            dst_ref=near.at[2 - 2 * h, me],
            send_sem=halo_send.at[h, n],
            recv_sem=halo_recv.at[me],
            device_id=member(row - 1 + 2 * h, 2 * n + 1 - h),
            device_id_type=MESH,
        )

    def halo_take(number):
        pltpu.make_async_remote_copy(
            src_ref=near.at[1, number],
            dst_ref=near.at[2 * core, number],
            send_sem=halo_send.at[0, 0],
            recv_sem=halo_recv.at[number],
            device_id=member(side_row, number),
            device_id_type=MESH,
        ).wait_recv()

    @pl.when(has_below)
    def _():
        for n in range(2):
            halo_copy(0, n).start()

    @pl.when(has_above)
    def _():
        for n in range(2):
            halo_copy(1, n).start()

    def ring_copy(slot, places, h, part):
        return pltpu.make_async_remote_copy(
            src_ref=near.at[h + 1 - core, me],
            dst_ref=ring.at[slot - 1, part],
            send_sem=ring_send.at[slot - 1, h],
            recv_sem=ring_recv.at[slot - 1, part],
            device_id=along(places, h),
            device_id_type=MESH,
        )

    for slot, places in SPREAD:
        for h in range(2):
            started.append(ring_copy(slot, places, h, core))
            started[-1].start()

    def take(slot, part):
        ring_copy(slot, 2, 0, part).wait_recv()

    def split_k(i, carry):
        for q in range(4):
            pairs = []
            for s in (4 * q, 4 * q + 2):
                second = k_buf[i, s + 1] if s + 1 < 15 else jnp.zeros((64, 64), F32)
                pairs.append(jnp.concatenate([k_buf[i, s], second], axis=1))
            both = jnp.concatenate(pairs, axis=1)
            high = both.astype(BF16)
            k_split[i, q, 0:64] = high
            k_split[i, q, 64:128] = (both - high.astype(F32)).astype(BF16)
        return carry

    def split_part(part):
        k_copies[part].wait()
        lax.fori_loop(4 * part, 4 * part + 4, split_k, 0)

    def place_group(side):
        empty = jnp.zeros((8, 128), F32)

        def place(m, carry):
            tiles = [[near[side, n, m * 3 + u] for u in range(3)] for n in range(4)]
            turned = [[swap_rows(tile) for tile in each] for each in tiles]
            for x in range(2):
                wholes = [[], []]
                for n in range(4):
                    upper = turned[n] if x else tiles[n]
                    under = tiles[n] if x else turned[n]
                    if side == 1:
                        found = [jnp.where(top, 0.0, under[0]), jnp.where(top, upper[1], under[2])]
                    else:
                        found = [jnp.where(top, upper[0], under[1]), jnp.where(top, upper[2], 0.0)]
                    ahead, behind = [empty] * (side // 2), [empty] * (2 - side // 2)
                    wholes[0] += ahead + found + behind
                    wholes[1] += ahead + [swap_lanes(tile) for tile in found] + behind
                for flipped in range(2):
                    whole = jnp.concatenate(wholes[flipped], axis=0)
                    high = whole.astype(BF16)
                    entry_at = 8 * side + 4 * m + 2 * x + flipped
                    table[entry_at, 0] = high
                    table[entry_at, 1] = (whole - high.astype(F32)).astype(BF16)
            return carry

        lax.fori_loop(0, 2, place, 0)

    split_part(0)
    split_part(1)
    table[24:26] = jnp.zeros((2, 2, 128, 128), BF16)
    pair_copy(0, odd * 2 + 1 - core, core, pair_peers[0]).wait_recv()
    for n in range(2):
        pair_copy(0, (1 - odd) * 2 + n, core, pair_peers[0]).wait_recv()
    place_group(1)

    @pl.when(has_side)
    def _():
        for number in range(4):
            halo_take(number)

    place_group(0)
    place_group(2)
    copies[2].wait()

    def entry(i, s):
        if s >= 15:
            return 24
        block = k_cols[AGG * core + i, s]
        place_of = block - (first_row + AGG * core - AGG)
        inside = (block >= 0) & (block < total_rows) & (place_of >= 0) & (place_of < 24)
        return jnp.where(inside, place_of, 24)

    low_16 = lax.broadcasted_iota(jnp.int32, (128, 128), 1) < 64

    def multiply_row(i):
        total = None
        for q in range(4):
            sides = []
            for s in (4 * q, 4 * q + 2):
                even = entry(i, s)
                other = lax.bitwise_xor(entry(i, s + 1), 1)
                parts = [jnp.where(low_16, table[even, part], table[other, part]) for part in range(2)]
                sides.append(jnp.concatenate(parts, axis=0))
            term = lax.dot_general(
                k_split[i, q],
                jnp.concatenate(sides, axis=1),
                (((1,), (1,)), ((), ())),
                preferred_element_type=F32,
            )
            total = term if total is None else total + term
        return total[0:64, 0:128] + total[0:64, 128:256] + total[64:128, 0:128]

    def multiply(n, carry):
        i = n + 2 * (n // 2)
        rows = pl.ds(pl.multiple_of(64 * n, 64), 64)
        for x in range(2):
            value = multiply_row(i + 2 * x)
            high = value.astype(BF16)
            weights[rows, 128 * x : 128 * x + 128] = high
            weights[rows, 256 + 128 * x : 384 + 128 * x] = (value - high.astype(F32)).astype(BF16)
        return carry

    lax.fori_loop(0, 4, multiply, 0)

    def prepare(place_at, slot):
        for part in range(2):

            def tile(m, u):
                return near[1, odd * 2 + part, m * 3 + u] if slot == 0 else ring[slot - 1, part, m * 3 + u]

            whole = jnp.concatenate(
                [jnp.concatenate([tile(m, u) for m in range(2)], axis=1) for u in range(3)], axis=0
            )
            rest = whole - whole.astype(BF16).astype(F32)
            rows = pl.ds(96 * place_at + 48 * part, 48)
            left_side[rows] = jnp.concatenate([whole, rest], axis=0).astype(BF16)

    def products(first, slots):
        count = len(slots)
        result = lax.dot_general(
            left_side[pl.ds(96 * first, 96 * count)],
            weights[...],
            (((1,), (0,)), ((), ())),
            preferred_element_type=F32,
        )
        for n, slot in enumerate(slots):
            for u in range(3):
                folded = []
                for part in range(2):
                    a = 96 * n + 48 * part + 8 * u
                    value = result[a : a + 8, 0:256] + result[a : a + 8, 256:512]
                    value = value + result[a + 24 : a + 32, 0:256]
                    folded.append(jnp.where(top, value[:, 0:128], value[:, 128:256]))
                value = jnp.where(top, folded[0], folded[1])
                value = value + swap_rows(jnp.where(top, folded[1], folded[0]))
                terms[u, slot] = value if u == 2 else pltpu.roll(value, 8 - 4 * u, 1)

    early, late = (0, 1), (2, 3)
    for part in range(2):
        take(1, part)
    for n, slot in enumerate(early):
        prepare(n, slot)
    products(0, early)
    for n, slot in enumerate(late):
        for part in range(2):
            take(slot, part)
        prepare(2 + n, slot)
    products(2, late)

    lane_group = lax.broadcasted_iota(jnp.int32, (8, 128), 1) // 32

    def rotate(value, groups):
        return value if groups % 4 == 0 else pltpu.roll(value, 32 * (groups % 4), 1)

    for u in (0, 2, 1):
        parts = [terms[u, slot] for slot in range(4)]
        for number in range(4):
            moved = [rotate(parts[slot], slot - number) for slot in range(4)]
            left_half = jnp.where(lane_group == 0, moved[0], moved[1])
            right_half = jnp.where(lane_group == 2, moved[2], moved[3])
            packed[number, u] = jnp.where(low, left_half, right_half)

    def side_copy(number):
        return pltpu.make_async_remote_copy(
            src_ref=packed.at[number, 2 * core],
            dst_ref=side_in.at[odd, 1 - core],
            send_sem=side_send.at[number],
            recv_sem=side_recv.at[odd, 1 - core],
            device_id=member(side_row, number),
            device_id_type=MESH,
        )

    def side_take(n, block):
        pltpu.make_async_remote_copy(
            src_ref=packed.at[0, 0],
            dst_ref=side_in.at[n, block],
            send_sem=side_send.at[0],
            recv_sem=side_recv.at[n, block],
            device_id=member(row - 1 + 2 * block, 2 * n + 1 - block),
            device_id_type=MESH,
        ).wait_recv()

    @pl.when(has_side)
    def _():
        for number in range(4):
            side_copy(number).start()

    def last_copy(n, number, chip, which, peer):
        return pltpu.make_async_remote_copy(
            src_ref=packed.at[number, pl.ds(1 - core, 2)],
            dst_ref=pair_in.at[chip, which],
            send_sem=pair_send.at[3 + n],
            recv_sem=last_recv.at[chip, which],
            device_id=peer,
            device_id_type=MESH,
        )

    for n, peer in enumerate(pair_peers):
        number = odd * 2 + 1 - core if n == 0 else (1 - odd) * 2 + n - 1
        started.append(last_copy(n, number, odd, core, peer))
        started[-1].start()
    pair_in[odd, core] = packed[me, pl.ds(1 - core, 2)]
    last_copy(0, 0, odd, 1 - core, pair_peers[0]).wait_recv()
    for n in range(2):
        last_copy(0, 0, 1 - odd, n, pair_peers[0]).wait_recv()

    @pl.when(has_below)
    def _():
        for n in range(2):
            side_take(n, 0)

    @pl.when(has_above)
    def _():
        for n in range(2):
            side_take(n, 1)

    for chip in range(2):
        totals = [pair_in[chip, 0, n] + pair_in[chip, 1, n] + side_in[chip, n] for n in range(2)]
        for slot in range(4):
            place_at = z - odd + chip + RING + (slot if chip else -slot)
            final[lax.rem(place_at, RING)] = jnp.where(
                lane_group == 0, rotate(totals[0], -slot), rotate(totals[1], 1 - slot)
            )
    turned = jnp.transpose(jnp.concatenate([final[n] for n in range(RING)], axis=0))
    for block in range(2):
        for band in range(7):
            a = 32 * block + 4 * band
            out[block, band] = turned[a : a + 4]

    for copy in started:
        copy.wait_send()

    @pl.when(has_below)
    def _():
        for n in range(2):
            halo_copy(0, n).wait_send()

    @pl.when(has_above)
    def _():
        for n in range(2):
            halo_copy(1, n).wait_send()

    @pl.when(has_side)
    def _():
        for number in range(4):
            side_copy(number).wait_send()


def body(row_count, k_vals, k_cols, p_vals, p_cols):
    own = k_vals.shape[0]
    dma = pltpu.SemaphoreType.DMA
    operands = [jnp.transpose(p_cols), k_cols, jnp.transpose(p_vals, (0, 1, 3, 2)), k_vals]
    result = pl.pallas_call(
        functools.partial(kernel, row_count),
        out_shape=jax.ShapeDtypeStruct((2, 7, 4, 64), F32),
        in_specs=[pl.BlockSpec(memory_space=pltpu.HBM)] * 4,
        out_specs=pl.BlockSpec(memory_space=pltpu.VMEM),
        scratch_shapes=[
            pltpu.SMEM((3, own), jnp.int32),
            pltpu.SMEM((own, 15), jnp.int32),
            pltpu.VMEM((own, 3, 4, 64), F32),
            pltpu.VMEM((AGG, 15, 64, 64), F32),
            pltpu.VMEM((AGG, 4, 128, 256), BF16),
            pltpu.VMEM((3, 4, 6, 8, 128), F32),
            pltpu.VMEM((3, 2, 6, 8, 128), F32),
            pltpu.VMEM((26, 2, 128, 128), BF16),
            pltpu.VMEM((256, 512), BF16),
            pltpu.VMEM((384, 256), BF16),
            pltpu.VMEM((3, 4, 8, 128), F32),
            pltpu.VMEM((4, 3, 8, 128), F32),
            pltpu.VMEM((2, 2, 2, 8, 128), F32),
            pltpu.VMEM((2, 2, 8, 128), F32),
            pltpu.VMEM((RING, 8, 128), F32),
            dma((5,)),
            dma((3, 2)),
            dma((3, 2)),
            dma((6,)),
            dma((4,)),
            dma((2, 2)),
            dma((2, 2)),
            dma((4,)),
            dma((4,)),
            dma((2, 2)),
        ],
        compiler_params=pltpu.CompilerParams(
            collective_id=0, has_side_effects=True, vmem_limit_bytes=32 * 1024 * 1024
        ),
    )(*[pltpu.with_memory_space_constraint(operand, pltpu.HBM) for operand in operands])
    return jnp.transpose(result, (0, 1, 3, 2))


def solution(mesh):
    placed = (
        P("row", None, None, None),
        P("row", None),
        P("row", None, None, "col"),
        P("row", None),
    )
    return jax.shard_map(
        functools.partial(body, mesh.shape["row"]),
        mesh=mesh,
        in_specs=placed,
        out_specs=P("row", None, None, "col"),
        check_vma=False,
    )
```

```python
import functools

import jax
import jax.numpy as jnp
from jax import lax
from jax.experimental import pallas as pl
from jax.experimental.pallas import tpu as pltpu
from jax.sharding import PartitionSpec as P

AGG = 8
RING = 8
SPREAD = ((3, -3), (2, 2), (1, -1))
MESH = pl.DeviceIdType.MESH
F32 = jnp.float32
BF16 = jnp.bfloat16


def kernel(
    row_count,
    p_cols_hbm,
    k_cols_hbm,
    p_hbm,
    k_hbm,
    out,
    p_cols,
    k_cols,
    p_buf,
    k_buf,
    k_split,
    near,
    ring,
    table,
    weights,
    left_side,
    terms,
    packed,
    pair_in,
    side_in,
    final,
    local_sem,
    ring_send,
    ring_recv,
    pair_send,
    pair_recv,
    last_recv,
    halo_send,
    halo_recv,
    side_send,
    side_recv,
):
    row = lax.axis_index("row")
    col = lax.axis_index("col")
    z = lax.div(col, 2)
    core = lax.rem(col, 2)
    own_rows = 2 * AGG
    first_row = row * own_rows
    total_rows = row_count * own_rows
    blocks_all = total_rows // AGG
    has_above = row < row_count - 1
    has_below = row > 0
    lower = core == 0
    has_side = jnp.where(lower, row, row_count - 1 - row) > 0
    has_other = jnp.where(lower, row_count - 1 - row, row) > 0
    side_row = row - 1 + 2 * core
    other_row = row + 1 - 2 * core
    odd = lax.rem(z, 2)
    turn = 1 - 2 * odd
    me = odd * 2 + core

    def along(places, which):
        return (row, lax.rem(z + turn * places + RING, RING) * 2 + which)

    def member(at_row, number):
        return (at_row, (z - odd) * 2 + number)

    pair_peers = [(row, z * 2 + 1 - core), along(1, 0), along(1, 1)]

    copies = [
        pltpu.make_async_copy(p_hbm, p_buf, local_sem.at[0]),
        pltpu.make_async_copy(p_cols_hbm, p_cols, local_sem.at[1]),
        pltpu.make_async_copy(k_cols_hbm, k_cols, local_sem.at[2]),
    ]
    for copy in copies:
        copy.start()
    barrier = pltpu.get_barrier_semaphore()

    def greet(peer):
        pl.semaphore_signal(barrier, inc=1, device_id=peer, device_id_type=MESH)

    for peer in pair_peers:
        greet(peer)
    for places in (-1, 2, -2, -3):
        for which in range(2):
            greet(along(places, which))

    @pl.when(has_side)
    def _():
        for number in range(4):
            greet(member(side_row, number))

    @pl.when(has_other)
    def _():
        for n in range(2):
            greet(member(other_row, 2 * n + core))

    k_copies = []
    for part in range(2):
        k_copies.append(
            pltpu.make_async_copy(
                k_hbm.at[pl.ds(AGG * core + 4 * part, 4)], k_buf.at[pl.ds(4 * part, 4)], local_sem.at[3 + part]
            )
        )
        k_copies[-1].start()

    top = lax.broadcasted_iota(jnp.int32, (8, 128), 0) < 4
    low = lax.broadcasted_iota(jnp.int32, (8, 128), 1) < 64

    def swap_rows(value):
        return pltpu.roll(value, 4, 0)

    def swap_lanes(value):
        return pltpu.roll(value, 64, 1)

    copies[1].wait()
    copies[0].wait()

    def window(j, u):
        total = jnp.zeros((4, 64), F32)
        for t in range(3):
            block = p_cols[t, j]
            position = block - (2 * row + j // AGG) + 1
            position = jnp.where((block >= 0) & (block < blocks_all), position, -1)
            total = total + jnp.where(jnp.full((4, 64), position) == u, p_buf[j, t], 0.0)
        return total

    for h in range(2):
        for m in range(2):
            for u in range(3):
                halves = []
                for x in range(2):
                    j = AGG * h + 4 * m + 2 * x
                    halves.append(jnp.concatenate([window(j, u), window(j + 1, u)], axis=1))
                near[h + 1 - core, me, m * 3 + u] = jnp.concatenate(halves, axis=0)

    @pl.when(jnp.logical_not(has_side))
    def _():
        near[2 * core] = jnp.zeros((4, 6, 8, 128), F32)

    @pl.when(jnp.logical_not(has_below))
    def _():
        for n in range(2):
            side_in[n, 0] = jnp.zeros((8, 128), F32)

    @pl.when(jnp.logical_not(has_above))
    def _():
        for n in range(2):
            side_in[n, 1] = jnp.zeros((8, 128), F32)

    pl.semaphore_wait(barrier, jnp.where(has_side, 4, 0) + jnp.where(has_other, 2, 0) + 11)

    def pair_copy(n, number, which, peer):
        return pltpu.make_async_remote_copy(
            src_ref=near.at[pl.ds(1 - core, 2), number],
            dst_ref=near.at[pl.ds(1 - which, 2), number],
            send_sem=pair_send.at[n],
            recv_sem=pair_recv.at[number],
            device_id=peer,
            device_id_type=MESH,
        )

    started = []
    for n, peer in enumerate(pair_peers):
        started.append(pair_copy(n, me, 1 - core if n == 0 else n - 1, peer))
        started[-1].start()

    def halo_copy(h, n):
        return pltpu.make_async_remote_copy(
            src_ref=near.at[h + 1 - core, me],
            dst_ref=near.at[2 - 2 * h, me],
            send_sem=halo_send.at[h, n],
            recv_sem=halo_recv.at[me],
            device_id=member(row - 1 + 2 * h, 2 * n + 1 - h),
            device_id_type=MESH,
        )

    def halo_take(number):
        pltpu.make_async_remote_copy(
            src_ref=near.at[1, number],
            dst_ref=near.at[2 * core, number],
            send_sem=halo_send.at[0, 0],
            recv_sem=halo_recv.at[number],
            device_id=member(side_row, number),
            device_id_type=MESH,
        ).wait_recv()

    @pl.when(has_below)
    def _():
        for n in range(2):
            halo_copy(0, n).start()

    @pl.when(has_above)
    def _():
        for n in range(2):
            halo_copy(1, n).start()

    def ring_copy(slot, places, h, part):
        return pltpu.make_async_remote_copy(
            src_ref=near.at[h + 1 - core, me],
            dst_ref=ring.at[slot - 1, part],
            send_sem=ring_send.at[slot - 1, h],
            recv_sem=ring_recv.at[slot - 1, part],
            device_id=along(places, h),
            device_id_type=MESH,
        )

    for slot, places in SPREAD:
        for h in range(2):
            started.append(ring_copy(slot, places, h, core))
            started[-1].start()

    def take(slot, part):
        ring_copy(slot, 2, 0, part).wait_recv()

    def split_k(i, carry):
        for q in range(4):
            pairs = []
            for s in (4 * q, 4 * q + 2):
                second = k_buf[i, s + 1] if s + 1 < 15 else jnp.zeros((64, 64), F32)
                pairs.append(jnp.concatenate([k_buf[i, s], second], axis=1))
            both = jnp.concatenate(pairs, axis=1)
            high = both.astype(BF16)
            lanes = slice(256 * q, 256 * q + 256)
            k_split[i, 0:64, lanes] = high
            k_split[i, 64:128, lanes] = (both - high.astype(F32)).astype(BF16)
        return carry

    def split_part(part):
        k_copies[part].wait()
        lax.fori_loop(4 * part, 4 * part + 4, split_k, 0)

    def place_group(side):
        def place(m, carry):
            tiles = [[near[side, n, m * 3 + u] for u in range(3)] for n in range(4)]
            turned = [[swap_rows(tile) for tile in each] for each in tiles]

            def piece(index, x, under):
                n, u = index // 5, index % 5 - side
                if u < 0 or u > 2:
                    return None
                return (tiles if x == under else turned)[n][u]

            for x in range(2):
                wholes = [[], []]
                for at in range(10):
                    upper, under = piece(2 * at, x, 0), piece(2 * at + 1, x, 1)
                    if upper is None and under is None:
                        wholes[0].append(jnp.zeros((8, 128), F32))
                        wholes[1].append(jnp.zeros((8, 128), F32))
                    else:
                        tile = jnp.where(top, 0.0 if upper is None else upper, 0.0 if under is None else under)
                        wholes[0].append(tile)
                        wholes[1].append(swap_lanes(tile))
                for flipped in range(2):
                    whole = jnp.concatenate(wholes[flipped], axis=0)
                    high = whole.astype(BF16)
                    entry_at = 8 * side + 4 * m + 2 * x + flipped
                    table[entry_at, 0] = high
                    table[entry_at, 1] = (whole - high.astype(F32)).astype(BF16)
            return carry

        lax.fori_loop(0, 2, place, 0, unroll=True)

    split_part(0)
    split_part(1)
    table[24:26] = jnp.zeros((2, 2, 80, 128), BF16)
    pair_copy(0, odd * 2 + 1 - core, core, pair_peers[0]).wait_recv()
    for n in range(2):
        pair_copy(0, (1 - odd) * 2 + n, core, pair_peers[0]).wait_recv()
    place_group(1)

    @pl.when(lower)
    def _():
        place_group(2)

    @pl.when(jnp.logical_not(lower))
    def _():
        place_group(0)

    @pl.when(has_side)
    def _():
        for number in range(4):
            halo_take(number)

    @pl.when(lower)
    def _():
        place_group(0)

    @pl.when(jnp.logical_not(lower))
    def _():
        place_group(2)

    copies[2].wait()

    def entry(i, s):
        if s >= 15:
            return 24
        block = k_cols[AGG * core + i, s]
        place_of = block - (first_row + AGG * core - AGG)
        inside = (block >= 0) & (block < total_rows) & (place_of >= 0) & (place_of < 24)
        return jnp.where(inside, place_of, 24)

    low_16 = lax.broadcasted_iota(jnp.int32, (80, 128), 1) < 64
    blank = jnp.zeros((48, 128), BF16)

    def multiply_row(i):
        sides = []
        for s in range(0, 16, 2):
            even = entry(i, s)
            other = lax.bitwise_xor(entry(i, s + 1), 1)
            parts = [jnp.where(low_16, table[even, part], table[other, part]) for part in range(2)]
            sides.append(jnp.concatenate([parts[0], blank, parts[1], blank], axis=0))
        total = lax.dot_general(
            k_split[i],
            jnp.concatenate(sides, axis=1),
            (((1,), (1,)), ((), ())),
            preferred_element_type=F32,
        )
        return total[0:64, 0:128] + total[0:64, 128:256] + total[64:128, 0:128]

    def multiply(n, carry):
        i = n + 2 * (n // 2)
        rows = pl.ds(pl.multiple_of(64 * n, 64), 64)
        for x in range(2):
            value = multiply_row(i + 2 * x)
            high = value.astype(BF16)
            weights[rows, 128 * x : 128 * x + 128] = high
            weights[rows, 256 + 128 * x : 384 + 128 * x] = (value - high.astype(F32)).astype(BF16)
        return carry

    lax.fori_loop(0, 4, multiply, 0, unroll=True)

    def prepare(place_at, slot):
        for part in range(2):

            def tile(m, u):
                return near[1, odd * 2 + part, m * 3 + u] if slot == 0 else ring[slot - 1, part, m * 3 + u]

            whole = jnp.concatenate(
                [jnp.concatenate([tile(m, u) for m in range(2)], axis=1) for u in range(3)], axis=0
            )
            rest = whole - whole.astype(BF16).astype(F32)
            rows = pl.ds(96 * place_at + 48 * part, 48)
            left_side[rows] = jnp.concatenate([whole, rest], axis=0).astype(BF16)

    lane = lax.broadcasted_iota(jnp.int32, (8, 128), 1)
    lane_group = lane // 32

    def spread(value, u):
        start = 8 - 4 * u
        moved = [pltpu.roll(value, start + 12 * n, 1) if start + 12 * n else value for n in range(4)]
        first = jnp.where(lane_group == 0, moved[0], moved[1])
        second = jnp.where(lane_group == 2, moved[2], moved[3])
        within = lane % 32 - start
        return jnp.where((within >= 0) & (within < 20), jnp.where(lane < 64, first, second), 0.0)

    def products(first, slots):
        count = len(slots)
        result = lax.dot_general(
            left_side[pl.ds(96 * first, 96 * count)],
            weights[...],
            (((1,), (0,)), ((), ())),
            preferred_element_type=F32,
        )
        for n, slot in enumerate(slots):
            for u in range(3):
                folded = []
                for part in range(2):
                    a = 96 * n + 48 * part + 8 * u
                    value = result[a : a + 8, 0:256] + result[a : a + 8, 256:512]
                    value = value + result[a + 24 : a + 32, 0:256]
                    folded.append(jnp.where(top, value[:, 0:128], value[:, 128:256]))
                value = jnp.where(top, folded[0], folded[1])
                value = value + swap_rows(jnp.where(top, folded[1], folded[0]))
                terms[u, slot] = spread(value, u)

    early, late = (0, 1), (2, 3)
    for part in range(2):
        take(1, part)
    for n, slot in enumerate(early):
        prepare(n, slot)
    products(0, early)
    for n, slot in enumerate(late):
        for part in range(2):
            take(slot, part)
        prepare(2 + n, slot)
    products(2, late)

    def rotate(value, groups):
        return value if groups % 4 == 0 else pltpu.roll(value, 32 * (groups % 4), 1)

    for u in (0, 2, 1):
        parts = [terms[u, slot] for slot in range(4)]
        for number in range(4):
            moved = [rotate(parts[slot], slot - number) for slot in range(4)]
            left_half = jnp.where(lane_group == 0, moved[0], moved[1])
            right_half = jnp.where(lane_group == 2, moved[2], moved[3])
            packed[number, u] = jnp.where(low, left_half, right_half)

    def side_copy(number):
        return pltpu.make_async_remote_copy(
            src_ref=packed.at[number, 2 * core],
            dst_ref=side_in.at[odd, 1 - core],
            send_sem=side_send.at[number],
            recv_sem=side_recv.at[odd, 1 - core],
            device_id=member(side_row, number),
            device_id_type=MESH,
        )

    def side_take(n, block):
        pltpu.make_async_remote_copy(
            src_ref=packed.at[0, 0],
            dst_ref=side_in.at[n, block],
            send_sem=side_send.at[0],
            recv_sem=side_recv.at[n, block],
            device_id=member(row - 1 + 2 * block, 2 * n + 1 - block),
            device_id_type=MESH,
        ).wait_recv()

    @pl.when(has_side)
    def _():
        for number in range(4):
            side_copy(number).start()

    def last_copy(n, number, chip, which, peer):
        return pltpu.make_async_remote_copy(
            src_ref=packed.at[number, pl.ds(1 - core, 2)],
            dst_ref=pair_in.at[chip, which],
            send_sem=pair_send.at[3 + n],
            recv_sem=last_recv.at[chip, which],
            device_id=peer,
            device_id_type=MESH,
        )

    for n, peer in enumerate(pair_peers):
        number = odd * 2 + 1 - core if n == 0 else (1 - odd) * 2 + n - 1
        started.append(last_copy(n, number, odd, core, peer))
        started[-1].start()
    pair_in[odd, core] = packed[me, pl.ds(1 - core, 2)]
    last_copy(0, 0, odd, 1 - core, pair_peers[0]).wait_recv()
    for n in range(2):
        last_copy(0, 0, 1 - odd, n, pair_peers[0]).wait_recv()

    @pl.when(has_below)
    def _():
        for n in range(2):
            side_take(n, 0)

    @pl.when(has_above)
    def _():
        for n in range(2):
            side_take(n, 1)

    for chip in range(2):
        totals = [pair_in[chip, 0, n] + pair_in[chip, 1, n] + side_in[chip, n] for n in range(2)]
        for slot in range(4):
            place_at = z - odd + chip + RING + (slot if chip else -slot)
            final[lax.rem(place_at, RING)] = jnp.where(
                lane_group == 0, rotate(totals[0], -slot), rotate(totals[1], 1 - slot)
            )
    turned = jnp.transpose(jnp.concatenate([final[n] for n in range(RING)], axis=0))
    for block in range(2):
        for band in range(7):
            a = 32 * block + 4 * band
            out[block, band] = turned[a : a + 4]

    for copy in started:
        copy.wait_send()

    @pl.when(has_below)
    def _():
        for n in range(2):
            halo_copy(0, n).wait_send()

    @pl.when(has_above)
    def _():
        for n in range(2):
            halo_copy(1, n).wait_send()

    @pl.when(has_side)
    def _():
        for number in range(4):
            side_copy(number).wait_send()


def body(row_count, k_vals, k_cols, p_vals, p_cols):
    own = k_vals.shape[0]
    dma = pltpu.SemaphoreType.DMA
    operands = [jnp.transpose(p_cols), k_cols, jnp.transpose(p_vals, (0, 1, 3, 2)), k_vals]
    result = pl.pallas_call(
        functools.partial(kernel, row_count),
        out_shape=jax.ShapeDtypeStruct((2, 7, 4, 64), F32),
        in_specs=[pl.BlockSpec(memory_space=pltpu.HBM)] * 4,
        out_specs=pl.BlockSpec(memory_space=pltpu.VMEM),
        scratch_shapes=[
            pltpu.SMEM((3, own), jnp.int32),
            pltpu.SMEM((own, 15), jnp.int32),
            pltpu.VMEM((own, 3, 4, 64), F32),
            pltpu.VMEM((AGG, 15, 64, 64), F32),
            pltpu.VMEM((AGG, 128, 1024), BF16),
            pltpu.VMEM((3, 4, 6, 8, 128), F32),
            pltpu.VMEM((3, 2, 6, 8, 128), F32),
            pltpu.VMEM((26, 2, 80, 128), BF16),
            pltpu.VMEM((256, 512), BF16),
            pltpu.VMEM((384, 256), BF16),
            pltpu.VMEM((3, 4, 8, 128), F32),
            pltpu.VMEM((4, 3, 8, 128), F32),
            pltpu.VMEM((2, 2, 2, 8, 128), F32),
            pltpu.VMEM((2, 2, 8, 128), F32),
            pltpu.VMEM((RING, 8, 128), F32),
            dma((5,)),
            dma((3, 2)),
            dma((3, 2)),
            dma((6,)),
            dma((4,)),
            dma((2, 2)),
            dma((2, 2)),
            dma((4,)),
            dma((4,)),
            dma((2, 2)),
        ],
        compiler_params=pltpu.CompilerParams(
            collective_id=0, has_side_effects=True, vmem_limit_bytes=32 * 1024 * 1024
        ),
    )(*[pltpu.with_memory_space_constraint(operand, pltpu.HBM) for operand in operands])
    return jnp.transpose(result, (0, 1, 3, 2))


def solution(mesh):
    placed = (
        P("row", None, None, None),
        P("row", None),
        P("row", None, None, "col"),
        P("row", None),
    )
    return jax.shard_map(
        functools.partial(body, mesh.shape["row"]),
        mesh=mesh,
        in_specs=placed,
        out_specs=P("row", None, None, "col"),
        check_vma=False,
    )
```

```python
import functools

import jax
import jax.numpy as jnp
from jax import lax
from jax.experimental import pallas as pl
from jax.experimental.pallas import tpu as pltpu
from jax.sharding import PartitionSpec as P

AGG = 8
RING = 8
SPREAD = ((3, -3), (2, 2), (1, -1))
MESH = pl.DeviceIdType.MESH
F32 = jnp.float32
BF16 = jnp.bfloat16


def kernel(
    row_count,
    p_cols_hbm,
    k_cols_hbm,
    p_hbm,
    k_hbm,
    out,
    p_cols,
    k_cols,
    p_buf,
    k_buf,
    k_split,
    near,
    ring,
    table,
    weights,
    terms,
    packed,
    pair_in,
    side_in,
    final,
    local_sem,
    ring_send,
    ring_recv,
    pair_send,
    pair_recv,
    last_recv,
    halo_send,
    halo_recv,
    side_send,
    side_recv,
):
    row = lax.axis_index("row")
    col = lax.axis_index("col")
    z = lax.div(col, 2)
    core = lax.rem(col, 2)
    own_rows = 2 * AGG
    first_row = row * own_rows
    total_rows = row_count * own_rows
    blocks_all = total_rows // AGG
    has_above = row < row_count - 1
    has_below = row > 0
    lower = core == 0
    has_side = jnp.where(lower, row, row_count - 1 - row) > 0
    has_other = jnp.where(lower, row_count - 1 - row, row) > 0
    side_row = row - 1 + 2 * core
    other_row = row + 1 - 2 * core
    odd = lax.rem(z, 2)
    turn = 1 - 2 * odd
    me = odd * 2 + core

    def along(places, which):
        return (row, lax.rem(z + turn * places + RING, RING) * 2 + which)

    def member(at_row, number):
        return (at_row, (z - odd) * 2 + number)

    pair_peers = [(row, z * 2 + 1 - core), along(1, 0), along(1, 1)]

    copies = [
        pltpu.make_async_copy(p_hbm, p_buf, local_sem.at[0]),
        pltpu.make_async_copy(p_cols_hbm, p_cols, local_sem.at[1]),
        pltpu.make_async_copy(k_cols_hbm, k_cols, local_sem.at[2]),
    ]
    for copy in copies:
        copy.start()
    barrier = pltpu.get_barrier_semaphore()

    def greet(peer):
        pl.semaphore_signal(barrier, inc=1, device_id=peer, device_id_type=MESH)

    for peer in pair_peers:
        greet(peer)
    for places in (-1, 2, -2, -3):
        for which in range(2):
            greet(along(places, which))

    @pl.when(has_side)
    def _():
        for number in range(4):
            greet(member(side_row, number))

    @pl.when(has_other)
    def _():
        for n in range(2):
            greet(member(other_row, 2 * n + core))

    k_copies = []
    for part in range(2):
        k_copies.append(
            pltpu.make_async_copy(
                k_hbm.at[pl.ds(AGG * core + 4 * part, 4)], k_buf.at[pl.ds(4 * part, 4)], local_sem.at[3 + part]
            )
        )
        k_copies[-1].start()

    top = lax.broadcasted_iota(jnp.int32, (8, 128), 0) < 4
    low = lax.broadcasted_iota(jnp.int32, (8, 128), 1) < 64

    def swap_rows(value):
        return pltpu.roll(value, 4, 0)

    def swap_lanes(value):
        return pltpu.roll(value, 64, 1)

    copies[1].wait()
    copies[0].wait()

    def window(j, u):
        total = jnp.zeros((4, 64), F32)
        for t in range(3):
            block = p_cols[t, j]
            position = block - (2 * row + j // AGG) + 1
            position = jnp.where((block >= 0) & (block < blocks_all), position, -1)
            total = total + jnp.where(jnp.full((4, 64), position) == u, p_buf[j, t], 0.0)
        return total

    for h in range(2):
        for m in range(2):
            for u in range(3):
                halves = []
                for x in range(2):
                    j = AGG * h + 4 * m + 2 * x
                    halves.append(jnp.concatenate([window(j, u), window(j + 1, u)], axis=1))
                near[h + 1 - core, me, m * 3 + u] = jnp.concatenate(halves, axis=0)

    @pl.when(jnp.logical_not(has_side))
    def _():
        near[2 * core] = jnp.zeros((4, 6, 8, 128), F32)

    @pl.when(jnp.logical_not(has_below))
    def _():
        for n in range(2):
            side_in[n, 0] = jnp.zeros((8, 128), F32)

    @pl.when(jnp.logical_not(has_above))
    def _():
        for n in range(2):
            side_in[n, 1] = jnp.zeros((8, 128), F32)

    pl.semaphore_wait(barrier, jnp.where(has_side, 4, 0) + jnp.where(has_other, 2, 0) + 11)

    def pair_copy(n, number, which, peer):
        return pltpu.make_async_remote_copy(
            src_ref=near.at[pl.ds(1 - core, 2), number],
            dst_ref=near.at[pl.ds(1 - which, 2), number],
            send_sem=pair_send.at[n],
            recv_sem=pair_recv.at[number],
            device_id=peer,
            device_id_type=MESH,
        )

    started = []
    for n, peer in enumerate(pair_peers):
        started.append(pair_copy(n, me, 1 - core if n == 0 else n - 1, peer))
        started[-1].start()

    def halo_copy(h, n):
        return pltpu.make_async_remote_copy(
            src_ref=near.at[h + 1 - core, me],
            dst_ref=near.at[2 - 2 * h, me],
            send_sem=halo_send.at[h, n],
            recv_sem=halo_recv.at[me],
            device_id=member(row - 1 + 2 * h, 2 * n + 1 - h),
            device_id_type=MESH,
        )

    def halo_take(number):
        pltpu.make_async_remote_copy(
            src_ref=near.at[1, number],
            dst_ref=near.at[2 * core, number],
            send_sem=halo_send.at[0, 0],
            recv_sem=halo_recv.at[number],
            device_id=member(side_row, number),
            device_id_type=MESH,
        ).wait_recv()

    @pl.when(has_below)
    def _():
        for n in range(2):
            halo_copy(0, n).start()

    @pl.when(has_above)
    def _():
        for n in range(2):
            halo_copy(1, n).start()

    def ring_copy(slot, places, h, part):
        return pltpu.make_async_remote_copy(
            src_ref=near.at[h + 1 - core, me],
            dst_ref=ring.at[slot - 1, part],
            send_sem=ring_send.at[slot - 1, h],
            recv_sem=ring_recv.at[slot - 1, part],
            device_id=along(places, h),
            device_id_type=MESH,
        )

    for slot, places in SPREAD:
        for h in range(2):
            started.append(ring_copy(slot, places, h, core))
            started[-1].start()

    def take(slot, part):
        ring_copy(slot, 2, 0, part).wait_recv()

    def split_k(i, carry):
        for q in range(4):
            pairs = []
            for s in (4 * q, 4 * q + 2):
                second = k_buf[i, s + 1] if s + 1 < 15 else jnp.zeros((64, 64), F32)
                pairs.append(jnp.concatenate([k_buf[i, s], second], axis=1))
            both = jnp.concatenate(pairs, axis=1)
            high = both.astype(BF16)
            lanes = slice(256 * q, 256 * q + 256)
            k_split[i, 0:64, lanes] = high
            k_split[i, 64:128, lanes] = (both - high.astype(F32)).astype(BF16)
        return carry

    def split_part(part):
        k_copies[part].wait()
        lax.fori_loop(4 * part, 4 * part + 4, split_k, 0)

    def place_group(side):
        def place(m, carry):
            tiles = [[near[side, n, m * 3 + u] for u in range(3)] for n in range(4)]
            turned = [[swap_rows(tile) for tile in each] for each in tiles]

            def piece(index, x, under):
                n, u = index // 5, index % 5 - side
                if u < 0 or u > 2:
                    return None
                return (tiles if x == under else turned)[n][u]

            for x in range(2):
                wholes = [[], []]
                for at in range(10):
                    upper, under = piece(2 * at, x, 0), piece(2 * at + 1, x, 1)
                    if upper is None and under is None:
                        wholes[0].append(jnp.zeros((8, 128), F32))
                        wholes[1].append(jnp.zeros((8, 128), F32))
                    else:
                        tile = jnp.where(top, 0.0 if upper is None else upper, 0.0 if under is None else under)
                        wholes[0].append(tile)
                        wholes[1].append(swap_lanes(tile))
                for flipped in range(2):
                    whole = jnp.concatenate(wholes[flipped], axis=0)
                    high = whole.astype(BF16)
                    entry_at = 8 * side + 4 * m + 2 * x + flipped
                    table[entry_at, 0] = high
                    table[entry_at, 1] = (whole - high.astype(F32)).astype(BF16)
            return carry

        lax.fori_loop(0, 2, place, 0, unroll=True)

    split_part(0)
    split_part(1)
    table[24:26] = jnp.zeros((2, 2, 80, 128), BF16)
    pair_copy(0, odd * 2 + 1 - core, core, pair_peers[0]).wait_recv()
    for n in range(2):
        pair_copy(0, (1 - odd) * 2 + n, core, pair_peers[0]).wait_recv()
    place_group(1)

    @pl.when(lower)
    def _():
        place_group(2)

    @pl.when(jnp.logical_not(lower))
    def _():
        place_group(0)

    @pl.when(has_side)
    def _():
        for number in range(4):
            halo_take(number)

    @pl.when(lower)
    def _():
        place_group(0)

    @pl.when(jnp.logical_not(lower))
    def _():
        place_group(2)

    copies[2].wait()

    def entry(i, s):
        if s >= 15:
            return 24
        block = k_cols[AGG * core + i, s]
        place_of = block - (first_row + AGG * core - AGG)
        inside = (block >= 0) & (block < total_rows) & (place_of >= 0) & (place_of < 24)
        return jnp.where(inside, place_of, 24)

    low_16 = lax.broadcasted_iota(jnp.int32, (80, 128), 1) < 64
    blank = jnp.zeros((48, 128), BF16)

    def multiply_row(i):
        sides = []
        for s in range(0, 16, 2):
            even = entry(i, s)
            other = lax.bitwise_xor(entry(i, s + 1), 1)
            parts = [jnp.where(low_16, table[even, part], table[other, part]) for part in range(2)]
            sides.append(jnp.concatenate([parts[0], blank, parts[1], blank], axis=0))
        total = lax.dot_general(
            k_split[i],
            jnp.concatenate(sides, axis=1),
            (((1,), (1,)), ((), ())),
            preferred_element_type=F32,
        )
        return total[0:64, 0:128] + total[0:64, 128:256] + total[64:128, 0:128]

    def multiply(n, carry):
        i = n + 2 * (n // 2)
        rows = pl.ds(pl.multiple_of(64 * n, 64), 64)
        for x in range(2):
            value = multiply_row(i + 2 * x)
            high = value.astype(BF16)
            weights[rows, 128 * x : 128 * x + 128] = high
            weights[rows, 256 + 128 * x : 384 + 128 * x] = (value - high.astype(F32)).astype(BF16)
        return carry

    lax.fori_loop(0, 4, multiply, 0, unroll=True)

    def prepare(slot):
        parts = []
        for part in range(2):

            def tile(m, u):
                return near[1, odd * 2 + part, m * 3 + u] if slot == 0 else ring[slot - 1, part, m * 3 + u]

            whole = jnp.concatenate(
                [jnp.concatenate([tile(m, u) for m in range(2)], axis=1) for u in range(3)], axis=0
            )
            parts += [whole, whole - whole.astype(BF16).astype(F32)]
        return jnp.concatenate(parts, axis=0).astype(BF16)

    lane = lax.broadcasted_iota(jnp.int32, (8, 128), 1)
    lane_group = lane // 32

    def spread(value, u):
        start = 8 - 4 * u
        moved = [pltpu.roll(value, start + 12 * n, 1) if start + 12 * n else value for n in range(4)]
        first = jnp.where(lane_group == 0, moved[0], moved[1])
        second = jnp.where(lane_group == 2, moved[2], moved[3])
        within = lane % 32 - start
        return jnp.where((within >= 0) & (within < 20), jnp.where(lane < 64, first, second), 0.0)

    def products(slots, factors):
        result = lax.dot_general(
            jnp.concatenate(factors, axis=0),
            weights[...],
            (((1,), (0,)), ((), ())),
            preferred_element_type=F32,
        )
        for n, slot in enumerate(slots):
            for u in range(3):
                folded = []
                for part in range(2):
                    a = 96 * n + 48 * part + 8 * u
                    value = result[a : a + 8, 0:256] + result[a : a + 8, 256:512]
                    value = value + result[a + 24 : a + 32, 0:256]
                    folded.append(jnp.where(top, value[:, 0:128], value[:, 128:256]))
                value = jnp.where(top, folded[0], folded[1])
                value = value + swap_rows(jnp.where(top, folded[1], folded[0]))
                terms[u, slot] = spread(value, u)

    factors = []
    for slot in range(4):
        for part in range(2):
            if slot > 0:
                take(slot, part)
        factors.append(prepare(slot))
    products((0, 1, 2, 3), factors)

    def rotate(value, groups):
        return value if groups % 4 == 0 else pltpu.roll(value, 32 * (groups % 4), 1)

    def pack(u):
        parts = [terms[u, slot] for slot in range(4)]
        for number in range(4):
            moved = [rotate(parts[slot], slot - number) for slot in range(4)]
            left_half = jnp.where(lane_group == 0, moved[0], moved[1])
            right_half = jnp.where(lane_group == 2, moved[2], moved[3])
            packed[number, u] = jnp.where(low, left_half, right_half)

    pack(0)
    pack(2)

    def side_copy(number):
        return pltpu.make_async_remote_copy(
            src_ref=packed.at[number, 2 * core],
            dst_ref=side_in.at[odd, 1 - core],
            send_sem=side_send.at[number],
            recv_sem=side_recv.at[odd, 1 - core],
            device_id=member(side_row, number),
            device_id_type=MESH,
        )

    def side_take(n, block):
        pltpu.make_async_remote_copy(
            src_ref=packed.at[0, 0],
            dst_ref=side_in.at[n, block],
            send_sem=side_send.at[0],
            recv_sem=side_recv.at[n, block],
            device_id=member(row - 1 + 2 * block, 2 * n + 1 - block),
            device_id_type=MESH,
        ).wait_recv()

    @pl.when(has_side)
    def _():
        for number in range(4):
            side_copy(number).start()

    pack(1)

    def last_copy(n, number, chip, which, peer):
        return pltpu.make_async_remote_copy(
            src_ref=packed.at[number, pl.ds(1 - core, 2)],
            dst_ref=pair_in.at[chip, which],
            send_sem=pair_send.at[3 + n],
            recv_sem=last_recv.at[chip, which],
            device_id=peer,
            device_id_type=MESH,
        )

    for n, peer in enumerate(pair_peers):
        number = odd * 2 + 1 - core if n == 0 else (1 - odd) * 2 + n - 1
        started.append(last_copy(n, number, odd, core, peer))
        started[-1].start()
    pair_in[odd, core] = packed[me, pl.ds(1 - core, 2)]
    last_copy(0, 0, odd, 1 - core, pair_peers[0]).wait_recv()
    for n in range(2):
        last_copy(0, 0, 1 - odd, n, pair_peers[0]).wait_recv()

    @pl.when(has_below)
    def _():
        for n in range(2):
            side_take(n, 0)

    @pl.when(has_above)
    def _():
        for n in range(2):
            side_take(n, 1)

    for chip in range(2):
        totals = [pair_in[chip, 0, n] + pair_in[chip, 1, n] + side_in[chip, n] for n in range(2)]
        for slot in range(4):
            place_at = z - odd + chip + RING + (slot if chip else -slot)
            final[lax.rem(place_at, RING)] = jnp.where(
                lane_group == 0, rotate(totals[0], -slot), rotate(totals[1], 1 - slot)
            )
    turned = jnp.transpose(jnp.concatenate([final[n] for n in range(RING)], axis=0))
    for block in range(2):
        for band in range(7):
            a = 32 * block + 4 * band
            out[block, band] = turned[a : a + 4]

    for copy in started:
        copy.wait_send()

    @pl.when(has_below)
    def _():
        for n in range(2):
            halo_copy(0, n).wait_send()

    @pl.when(has_above)
    def _():
        for n in range(2):
            halo_copy(1, n).wait_send()

    @pl.when(has_side)
    def _():
        for number in range(4):
            side_copy(number).wait_send()


def body(row_count, k_vals, k_cols, p_vals, p_cols):
    own = k_vals.shape[0]
    dma = pltpu.SemaphoreType.DMA
    operands = [jnp.transpose(p_cols), k_cols, jnp.transpose(p_vals, (0, 1, 3, 2)), k_vals]
    result = pl.pallas_call(
        functools.partial(kernel, row_count),
        out_shape=jax.ShapeDtypeStruct((2, 7, 4, 64), F32),
        in_specs=[pl.BlockSpec(memory_space=pltpu.HBM)] * 4,
        out_specs=pl.BlockSpec(memory_space=pltpu.VMEM),
        scratch_shapes=[
            pltpu.SMEM((3, own), jnp.int32),
            pltpu.SMEM((own, 15), jnp.int32),
            pltpu.VMEM((own, 3, 4, 64), F32),
            pltpu.VMEM((AGG, 15, 64, 64), F32),
            pltpu.VMEM((AGG, 128, 1024), BF16),
            pltpu.VMEM((3, 4, 6, 8, 128), F32),
            pltpu.VMEM((3, 2, 6, 8, 128), F32),
            pltpu.VMEM((26, 2, 80, 128), BF16),
            pltpu.VMEM((256, 512), BF16),
            pltpu.VMEM((3, 4, 8, 128), F32),
            pltpu.VMEM((4, 3, 8, 128), F32),
            pltpu.VMEM((2, 2, 2, 8, 128), F32),
            pltpu.VMEM((2, 2, 8, 128), F32),
            pltpu.VMEM((RING, 8, 128), F32),
            dma((5,)),
            dma((3, 2)),
            dma((3, 2)),
            dma((6,)),
            dma((4,)),
            dma((2, 2)),
            dma((2, 2)),
            dma((4,)),
            dma((4,)),
            dma((2, 2)),
        ],
        compiler_params=pltpu.CompilerParams(
            collective_id=0, has_side_effects=True, vmem_limit_bytes=32 * 1024 * 1024
        ),
    )(*[pltpu.with_memory_space_constraint(operand, pltpu.HBM) for operand in operands])
    return jnp.transpose(result, (0, 1, 3, 2))


def solution(mesh):
    placed = (
        P("row", None, None, None),
        P("row", None),
        P("row", None, None, "col"),
        P("row", None),
    )
    return jax.shard_map(
        functools.partial(body, mesh.shape["row"]),
        mesh=mesh,
        in_specs=placed,
        out_specs=P("row", None, None, "col"),
        check_vma=False,
    )
```

```python
import functools

import jax
import jax.numpy as jnp
from jax import lax
from jax.experimental import pallas as pl
from jax.experimental.pallas import tpu as pltpu
from jax.sharding import PartitionSpec as P

AGG = 8
RING = 8
SPREAD = ((3, -3), (2, 2), (1, -1))
MESH = pl.DeviceIdType.MESH
F32 = jnp.float32
BF16 = jnp.bfloat16


def kernel(
    row_count,
    p_cols_hbm,
    k_cols_hbm,
    p_hbm,
    k_hbm,
    out,
    p_cols,
    k_cols,
    p_buf,
    k_buf,
    k_split,
    near,
    ring,
    table,
    weights,
    terms,
    packed,
    pair_in,
    side_in,
    final,
    local_sem,
    ring_send,
    ring_recv,
    pair_send,
    pair_recv,
    last_recv,
    halo_send,
    halo_recv,
    side_send,
    side_recv,
):
    row = lax.axis_index("row")
    col = lax.axis_index("col")
    z = lax.div(col, 2)
    core = lax.rem(col, 2)
    own_rows = 2 * AGG
    first_row = row * own_rows
    total_rows = row_count * own_rows
    blocks_all = total_rows // AGG
    has_above = row < row_count - 1
    has_below = row > 0
    lower = core == 0
    has_side = jnp.where(lower, row, row_count - 1 - row) > 0
    has_other = jnp.where(lower, row_count - 1 - row, row) > 0
    side_row = row - 1 + 2 * core
    other_row = row + 1 - 2 * core
    odd = lax.rem(z, 2)
    turn = 1 - 2 * odd
    me = odd * 2 + core

    def along(places, which):
        return (row, lax.rem(z + turn * places + RING, RING) * 2 + which)

    def member(at_row, number):
        return (at_row, (z - odd) * 2 + number)

    pair_peers = [(row, z * 2 + 1 - core), along(1, 0), along(1, 1)]

    copies = [
        pltpu.make_async_copy(p_hbm, p_buf, local_sem.at[0]),
        pltpu.make_async_copy(p_cols_hbm, p_cols, local_sem.at[1]),
        pltpu.make_async_copy(k_cols_hbm, k_cols, local_sem.at[2]),
    ]
    for copy in copies:
        copy.start()
    barrier = pltpu.get_barrier_semaphore()

    def greet(peer):
        pl.semaphore_signal(barrier, inc=1, device_id=peer, device_id_type=MESH)

    for peer in pair_peers:
        greet(peer)
    for places in (-1, 2, -2, -3):
        for which in range(2):
            greet(along(places, which))

    @pl.when(has_side)
    def _():
        for number in range(4):
            greet(member(side_row, number))

    @pl.when(has_other)
    def _():
        for n in range(2):
            greet(member(other_row, 2 * n + core))

    k_copies = []
    for part in range(2):
        k_copies.append(
            pltpu.make_async_copy(
                k_hbm.at[pl.ds(AGG * core + 4 * part, 4)], k_buf.at[pl.ds(4 * part, 4)], local_sem.at[3 + part]
            )
        )
        k_copies[-1].start()

    top = lax.broadcasted_iota(jnp.int32, (8, 128), 0) < 4
    low = lax.broadcasted_iota(jnp.int32, (8, 128), 1) < 64

    def swap_rows(value):
        return pltpu.roll(value, 4, 0)

    def swap_lanes(value):
        return pltpu.roll(value, 64, 1)

    copies[1].wait()
    copies[0].wait()

    def window(j, u):
        total = jnp.zeros((4, 64), F32)
        for t in range(3):
            block = p_cols[t, j]
            position = block - (2 * row + j // AGG) + 1
            position = jnp.where((block >= 0) & (block < blocks_all), position, -1)
            total = total + jnp.where(jnp.full((4, 64), position) == u, p_buf[j, t], 0.0)
        return total

    for h in range(2):
        for m in range(2):
            for u in range(3):
                halves = []
                for x in range(2):
                    j = AGG * h + 4 * m + 2 * x
                    halves.append(jnp.concatenate([window(j, u), window(j + 1, u)], axis=1))
                near[h + 1 - core, me, m * 3 + u] = jnp.concatenate(halves, axis=0)

    @pl.when(jnp.logical_not(has_side))
    def _():
        near[2 * core] = jnp.zeros((4, 6, 8, 128), F32)

    @pl.when(jnp.logical_not(has_below))
    def _():
        for n in range(2):
            side_in[n, 0] = jnp.zeros((8, 128), F32)

    @pl.when(jnp.logical_not(has_above))
    def _():
        for n in range(2):
            side_in[n, 1] = jnp.zeros((8, 128), F32)

    pl.semaphore_wait(barrier, jnp.where(has_side, 4, 0) + jnp.where(has_other, 2, 0) + 11)

    def pair_copy(n, number, which, peer):
        return pltpu.make_async_remote_copy(
            src_ref=near.at[pl.ds(1 - core, 2), number],
            dst_ref=near.at[pl.ds(1 - which, 2), number],
            send_sem=pair_send.at[n],
            recv_sem=pair_recv.at[number],
            device_id=peer,
            device_id_type=MESH,
        )

    started = []
    for n, peer in enumerate(pair_peers):
        started.append(pair_copy(n, me, 1 - core if n == 0 else n - 1, peer))
        started[-1].start()

    def halo_copy(h, n):
        return pltpu.make_async_remote_copy(
            src_ref=near.at[h + 1 - core, me],
            dst_ref=near.at[2 - 2 * h, me],
            send_sem=halo_send.at[h, n],
            recv_sem=halo_recv.at[me],
            device_id=member(row - 1 + 2 * h, 2 * n + 1 - h),
            device_id_type=MESH,
        )

    def halo_take(number):
        pltpu.make_async_remote_copy(
            src_ref=near.at[1, number],
            dst_ref=near.at[2 * core, number],
            send_sem=halo_send.at[0, 0],
            recv_sem=halo_recv.at[number],
            device_id=member(side_row, number),
            device_id_type=MESH,
        ).wait_recv()

    @pl.when(has_below)
    def _():
        for n in range(2):
            halo_copy(0, n).start()

    @pl.when(has_above)
    def _():
        for n in range(2):
            halo_copy(1, n).start()

    def ring_copy(slot, places, h, part):
        return pltpu.make_async_remote_copy(
            src_ref=near.at[h + 1 - core, me],
            dst_ref=ring.at[slot - 1, part],
            send_sem=ring_send.at[slot - 1, h],
            recv_sem=ring_recv.at[slot - 1, part],
            device_id=along(places, h),
            device_id_type=MESH,
        )

    for slot, places in SPREAD:
        for h in range(2):
            started.append(ring_copy(slot, places, h, core))
            started[-1].start()

    def take(slot, part):
        ring_copy(slot, 2, 0, part).wait_recv()

    def split_k(i, carry):
        for q in range(4):
            pairs = []
            for s in (4 * q, 4 * q + 2):
                second = k_buf[i, s + 1] if s + 1 < 15 else jnp.zeros((64, 64), F32)
                pairs.append(jnp.concatenate([k_buf[i, s], second], axis=1))
            both = jnp.concatenate(pairs, axis=1)
            high = both.astype(BF16)
            lanes = slice(256 * q, 256 * q + 256)
            k_split[i, 0:64, lanes] = high
            k_split[i, 64:128, lanes] = (both - high.astype(F32)).astype(BF16)
        return carry

    def split_part(part):
        k_copies[part].wait()
        lax.fori_loop(4 * part, 4 * part + 4, split_k, 0)

    def place_group(side):
        def place(m, carry):
            tiles = [[near[side, n, m * 3 + u] for u in range(3)] for n in range(4)]
            turned = [[swap_rows(tile) for tile in each] for each in tiles]

            def piece(index, x, under):
                n, u = index // 5, index % 5 - side
                if u < 0 or u > 2:
                    return None
                return (tiles if x == under else turned)[n][u]

            for x in range(2):
                wholes = [[], []]
                for at in range(10):
                    upper, under = piece(2 * at, x, 0), piece(2 * at + 1, x, 1)
                    if upper is None and under is None:
                        wholes[0].append(jnp.zeros((8, 128), F32))
                        wholes[1].append(jnp.zeros((8, 128), F32))
                    else:
                        tile = jnp.where(top, 0.0 if upper is None else upper, 0.0 if under is None else under)
                        wholes[0].append(tile)
                        wholes[1].append(swap_lanes(tile))
                for flipped in range(2):
                    whole = jnp.concatenate(wholes[flipped], axis=0)
                    high = whole.astype(BF16)
                    entry_at = 8 * side + 4 * m + 2 * x + flipped
                    table[entry_at, 0] = high
                    table[entry_at, 1] = (whole - high.astype(F32)).astype(BF16)
            return carry

        lax.fori_loop(0, 2, place, 0, unroll=True)

    split_part(0)
    split_part(1)
    table[24:26] = jnp.zeros((2, 2, 80, 128), BF16)
    pair_copy(0, odd * 2 + 1 - core, core, pair_peers[0]).wait_recv()
    for n in range(2):
        pair_copy(0, (1 - odd) * 2 + n, core, pair_peers[0]).wait_recv()
    place_group(1)

    @pl.when(lower)
    def _():
        place_group(2)

    @pl.when(jnp.logical_not(lower))
    def _():
        place_group(0)

    @pl.when(has_side)
    def _():
        for number in range(4):
            halo_take(number)

    @pl.when(lower)
    def _():
        place_group(0)

    @pl.when(jnp.logical_not(lower))
    def _():
        place_group(2)

    copies[2].wait()

    def entry(i, s):
        if s >= 15:
            return 24
        block = k_cols[AGG * core + i, s]
        place_of = block - (first_row + AGG * core - AGG)
        inside = (block >= 0) & (block < total_rows) & (place_of >= 0) & (place_of < 24)
        return jnp.where(inside, place_of, 24)

    low_16 = lax.broadcasted_iota(jnp.int32, (80, 128), 1) < 64
    blank = jnp.zeros((48, 128), BF16)

    def multiply_row(i):
        sides = []
        for s in range(0, 16, 2):
            even = entry(i, s)
            other = lax.bitwise_xor(entry(i, s + 1), 1)
            parts = [jnp.where(low_16, table[even, part], table[other, part]) for part in range(2)]
            sides.append(jnp.concatenate([parts[0], blank, parts[1], blank], axis=0))
        total = lax.dot_general(
            k_split[i],
            jnp.concatenate(sides, axis=1),
            (((1,), (1,)), ((), ())),
            preferred_element_type=F32,
        )
        return total[0:64, 0:128] + total[0:64, 128:256] + total[64:128, 0:128]

    def multiply(i, carry):
        rows = pl.ds(pl.multiple_of(64 * i, 64), 64)
        value = multiply_row(i)
        high = value.astype(BF16)
        weights[rows, 0:128] = high
        weights[rows, 128:256] = (value - high.astype(F32)).astype(BF16)
        return carry

    lax.fori_loop(0, AGG, multiply, 0, unroll=True)

    def merge(zero, one):
        mixed = swap_rows(jnp.where(top, one, zero))
        return [jnp.where(top, zero, mixed), jnp.where(top, mixed, one)]

    def prepare(slot):
        def tile(part, at):
            return near[1, odd * 2 + part, at] if slot == 0 else ring[slot - 1, part, at]

        rows = []
        for u in range(3):
            pieces = merge(tile(0, u), tile(1, u)) + merge(tile(0, 3 + u), tile(1, 3 + u))
            rows.append(jnp.concatenate(pieces, axis=1))
        whole = jnp.concatenate(rows, axis=0)
        return jnp.concatenate([whole, whole - whole.astype(BF16).astype(F32)], axis=0).astype(BF16)

    lane = lax.broadcasted_iota(jnp.int32, (8, 128), 1)
    lane_group = lane // 32

    def spread(value, u):
        start = 8 - 4 * u
        moved = [pltpu.roll(value, start + 12 * n, 1) if start + 12 * n else value for n in range(4)]
        first = jnp.where(lane_group == 0, moved[0], moved[1])
        second = jnp.where(lane_group == 2, moved[2], moved[3])
        within = lane % 32 - start
        return jnp.where((within >= 0) & (within < 20), jnp.where(lane < 64, first, second), 0.0)

    def products(slots, factors):
        result = lax.dot_general(
            jnp.concatenate(factors, axis=0),
            weights[...],
            (((1,), (0,)), ((), ())),
            preferred_element_type=F32,
        )
        for n, slot in enumerate(slots):
            for u in range(3):
                a = 48 * n + 8 * u
                value = result[a : a + 8, 0:128] + result[a : a + 8, 128:256] + result[a + 24 : a + 32, 0:128]
                terms[u, slot] = spread(value, u)

    factors = []
    for slot in range(4):
        for part in range(2):
            if slot > 0:
                take(slot, part)
        factors.append(prepare(slot))
    products((0, 1, 2, 3), factors)

    def rotate(value, groups):
        return value if groups % 4 == 0 else pltpu.roll(value, 32 * (groups % 4), 1)

    def pack(u):
        parts = [terms[u, slot] for slot in range(4)]
        for number in range(4):
            moved = [rotate(parts[slot], slot - number) for slot in range(4)]
            left_half = jnp.where(lane_group == 0, moved[0], moved[1])
            right_half = jnp.where(lane_group == 2, moved[2], moved[3])
            packed[number, u] = jnp.where(low, left_half, right_half)

    pack(0)
    pack(2)

    def side_copy(number):
        return pltpu.make_async_remote_copy(
            src_ref=packed.at[number, 2 * core],
            dst_ref=side_in.at[odd, 1 - core],
            send_sem=side_send.at[number],
            recv_sem=side_recv.at[odd, 1 - core],
            device_id=member(side_row, number),
            device_id_type=MESH,
        )

    def side_take(n, block):
        pltpu.make_async_remote_copy(
            src_ref=packed.at[0, 0],
            dst_ref=side_in.at[n, block],
            send_sem=side_send.at[0],
            recv_sem=side_recv.at[n, block],
            device_id=member(row - 1 + 2 * block, 2 * n + 1 - block),
            device_id_type=MESH,
        ).wait_recv()

    @pl.when(has_side)
    def _():
        for number in range(4):
            side_copy(number).start()

    pack(1)

    def last_copy(n, number, chip, which, peer):
        return pltpu.make_async_remote_copy(
            src_ref=packed.at[number, pl.ds(1 - core, 2)],
            dst_ref=pair_in.at[chip, which],
            send_sem=pair_send.at[3 + n],
            recv_sem=last_recv.at[chip, which],
            device_id=peer,
            device_id_type=MESH,
        )

    for n, peer in enumerate(pair_peers):
        number = odd * 2 + 1 - core if n == 0 else (1 - odd) * 2 + n - 1
        started.append(last_copy(n, number, odd, core, peer))
        started[-1].start()
    pair_in[odd, core] = packed[me, pl.ds(1 - core, 2)]
    last_copy(0, 0, odd, 1 - core, pair_peers[0]).wait_recv()
    for n in range(2):
        last_copy(0, 0, 1 - odd, n, pair_peers[0]).wait_recv()

    @pl.when(has_below)
    def _():
        for n in range(2):
            side_take(n, 0)

    @pl.when(has_above)
    def _():
        for n in range(2):
            side_take(n, 1)

    for chip in range(2):
        totals = [pair_in[chip, 0, n] + pair_in[chip, 1, n] + side_in[chip, n] for n in range(2)]
        for slot in range(4):
            place_at = z - odd + chip + RING + (slot if chip else -slot)
            final[lax.rem(place_at, RING)] = jnp.where(
                lane_group == 0, rotate(totals[0], -slot), rotate(totals[1], 1 - slot)
            )
    turned = jnp.transpose(jnp.concatenate([final[n] for n in range(RING)], axis=0))
    for block in range(2):
        for band in range(7):
            a = 32 * block + 4 * band
            out[block, band] = turned[a : a + 4]

    for copy in started:
        copy.wait_send()

    @pl.when(has_below)
    def _():
        for n in range(2):
            halo_copy(0, n).wait_send()

    @pl.when(has_above)
    def _():
        for n in range(2):
            halo_copy(1, n).wait_send()

    @pl.when(has_side)
    def _():
        for number in range(4):
            side_copy(number).wait_send()


def body(row_count, k_vals, k_cols, p_vals, p_cols):
    own = k_vals.shape[0]
    dma = pltpu.SemaphoreType.DMA
    operands = [jnp.transpose(p_cols), k_cols, jnp.transpose(p_vals, (0, 1, 3, 2)), k_vals]
    result = pl.pallas_call(
        functools.partial(kernel, row_count),
        out_shape=jax.ShapeDtypeStruct((2, 7, 4, 64), F32),
        in_specs=[pl.BlockSpec(memory_space=pltpu.HBM)] * 4,
        out_specs=pl.BlockSpec(memory_space=pltpu.VMEM),
        scratch_shapes=[
            pltpu.SMEM((3, own), jnp.int32),
            pltpu.SMEM((own, 15), jnp.int32),
            pltpu.VMEM((own, 3, 4, 64), F32),
            pltpu.VMEM((AGG, 15, 64, 64), F32),
            pltpu.VMEM((AGG, 128, 1024), BF16),
            pltpu.VMEM((3, 4, 6, 8, 128), F32),
            pltpu.VMEM((3, 2, 6, 8, 128), F32),
            pltpu.VMEM((26, 2, 80, 128), BF16),
            pltpu.VMEM((512, 256), BF16),
            pltpu.VMEM((3, 4, 8, 128), F32),
            pltpu.VMEM((4, 3, 8, 128), F32),
            pltpu.VMEM((2, 2, 2, 8, 128), F32),
            pltpu.VMEM((2, 2, 8, 128), F32),
            pltpu.VMEM((RING, 8, 128), F32),
            dma((5,)),
            dma((3, 2)),
            dma((3, 2)),
            dma((6,)),
            dma((4,)),
            dma((2, 2)),
            dma((2, 2)),
            dma((4,)),
            dma((4,)),
            dma((2, 2)),
        ],
        compiler_params=pltpu.CompilerParams(
            collective_id=0, has_side_effects=True, vmem_limit_bytes=32 * 1024 * 1024
        ),
    )(*[pltpu.with_memory_space_constraint(operand, pltpu.HBM) for operand in operands])
    return jnp.transpose(result, (0, 1, 3, 2))


def solution(mesh):
    placed = (
        P("row", None, None, None),
        P("row", None),
        P("row", None, None, "col"),
        P("row", None),
    )
    return jax.shard_map(
        functools.partial(body, mesh.shape["row"]),
        mesh=mesh,
        in_specs=placed,
        out_specs=P("row", None, None, "col"),
        check_vma=False,
    )
```

```python
import functools

import jax
import jax.numpy as jnp
from jax import lax
from jax.experimental import pallas as pl
from jax.experimental.pallas import tpu as pltpu
from jax.sharding import PartitionSpec as P

AGG = 8
RING = 8
SPREAD = ((3, -3), (2, 2), (1, -1))
MESH = pl.DeviceIdType.MESH
F32 = jnp.float32
BF16 = jnp.bfloat16


def kernel(
    row_count,
    p_cols_hbm,
    k_cols_hbm,
    p_hbm,
    k_hbm,
    out,
    p_cols,
    k_cols,
    p_buf,
    k_buf,
    k_split,
    near,
    ring,
    table,
    weights,
    terms,
    packed,
    pair_in,
    side_in,
    final,
    local_sem,
    ring_send,
    ring_recv,
    pair_send,
    pair_recv,
    last_recv,
    halo_send,
    halo_recv,
    side_send,
    side_recv,
):
    row = lax.axis_index("row")
    col = lax.axis_index("col")
    z = lax.div(col, 2)
    core = lax.rem(col, 2)
    own_rows = 2 * AGG
    first_row = row * own_rows
    total_rows = row_count * own_rows
    blocks_all = total_rows // AGG
    has_above = row < row_count - 1
    has_below = row > 0
    lower = core == 0
    has_side = jnp.where(lower, row, row_count - 1 - row) > 0
    has_other = jnp.where(lower, row_count - 1 - row, row) > 0
    side_row = row - 1 + 2 * core
    other_row = row + 1 - 2 * core
    odd = lax.rem(z, 2)
    turn = 1 - 2 * odd
    me = odd * 2 + core

    def along(places, which):
        return (row, lax.rem(z + turn * places + RING, RING) * 2 + which)

    def member(at_row, number):
        return (at_row, (z - odd) * 2 + number)

    pair_peers = [(row, z * 2 + 1 - core), along(1, 0), along(1, 1)]

    copies = [
        pltpu.make_async_copy(p_hbm, p_buf, local_sem.at[0]),
        pltpu.make_async_copy(p_cols_hbm, p_cols, local_sem.at[1]),
        pltpu.make_async_copy(k_cols_hbm, k_cols, local_sem.at[2]),
    ]
    for copy in copies:
        copy.start()
    barrier = pltpu.get_barrier_semaphore()

    def greet(peer):
        pl.semaphore_signal(barrier, inc=1, device_id=peer, device_id_type=MESH)

    for peer in pair_peers:
        greet(peer)
    for places in (-1, 2, -2, -3):
        for which in range(2):
            greet(along(places, which))

    @pl.when(has_side)
    def _():
        for number in range(4):
            greet(member(side_row, number))

    @pl.when(has_other)
    def _():
        for n in range(2):
            greet(member(other_row, 2 * n + core))

    k_copies = []
    for part in range(2):
        k_copies.append(
            pltpu.make_async_copy(
                k_hbm.at[pl.ds(AGG * core + 4 * part, 4)], k_buf.at[pl.ds(4 * part, 4)], local_sem.at[3 + part]
            )
        )
        k_copies[-1].start()

    top = lax.broadcasted_iota(jnp.int32, (8, 128), 0) < 4
    low = lax.broadcasted_iota(jnp.int32, (8, 128), 1) < 64

    def swap_rows(value):
        return pltpu.roll(value, 4, 0)

    def swap_lanes(value):
        return pltpu.roll(value, 64, 1)

    copies[1].wait()
    copies[0].wait()

    def window(j, u):
        total = jnp.zeros((4, 64), F32)
        for t in range(3):
            block = p_cols[t, j]
            position = block - (2 * row + j // AGG) + 1
            position = jnp.where((block >= 0) & (block < blocks_all), position, -1)
            total = total + jnp.where(jnp.full((4, 64), position) == u, p_buf[j, t], 0.0)
        return total

    for h in range(2):
        for m in range(2):
            for u in range(3):
                halves = []
                for x in range(2):
                    j = AGG * h + 4 * m + 2 * x
                    halves.append(jnp.concatenate([window(j, u), window(j + 1, u)], axis=1))
                near[h + 1 - core, me, m * 3 + u] = jnp.concatenate(halves, axis=0)

    @pl.when(jnp.logical_not(has_side))
    def _():
        near[2 * core] = jnp.zeros((4, 6, 8, 128), F32)

    @pl.when(jnp.logical_not(has_below))
    def _():
        for n in range(2):
            side_in[n, 0] = jnp.zeros((8, 128), F32)

    @pl.when(jnp.logical_not(has_above))
    def _():
        for n in range(2):
            side_in[n, 1] = jnp.zeros((8, 128), F32)

    pl.semaphore_wait(barrier, jnp.where(has_side, 4, 0) + jnp.where(has_other, 2, 0) + 11)

    def pair_copy(n, number, which, peer):
        return pltpu.make_async_remote_copy(
            src_ref=near.at[pl.ds(1 - core, 2), number],
            dst_ref=near.at[pl.ds(1 - which, 2), number],
            send_sem=pair_send.at[n],
            recv_sem=pair_recv.at[number],
            device_id=peer,
            device_id_type=MESH,
        )

    started = []
    for n, peer in enumerate(pair_peers):
        started.append(pair_copy(n, me, 1 - core if n == 0 else n - 1, peer))
        started[-1].start()

    def halo_copy(h, n):
        return pltpu.make_async_remote_copy(
            src_ref=near.at[h + 1 - core, me],
            dst_ref=near.at[2 - 2 * h, me],
            send_sem=halo_send.at[h, n],
            recv_sem=halo_recv.at[me],
            device_id=member(row - 1 + 2 * h, 2 * n + 1 - h),
            device_id_type=MESH,
        )

    def halo_take(number):
        pltpu.make_async_remote_copy(
            src_ref=near.at[1, number],
            dst_ref=near.at[2 * core, number],
            send_sem=halo_send.at[0, 0],
            recv_sem=halo_recv.at[number],
            device_id=member(side_row, number),
            device_id_type=MESH,
        ).wait_recv()

    @pl.when(has_below)
    def _():
        for n in range(2):
            halo_copy(0, n).start()

    @pl.when(has_above)
    def _():
        for n in range(2):
            halo_copy(1, n).start()

    def ring_copy(slot, places, h, part):
        return pltpu.make_async_remote_copy(
            src_ref=near.at[h + 1 - core, me],
            dst_ref=ring.at[slot - 1, part],
            send_sem=ring_send.at[slot - 1, h],
            recv_sem=ring_recv.at[slot - 1, part],
            device_id=along(places, h),
            device_id_type=MESH,
        )

    for slot, places in SPREAD:
        for h in range(2):
            started.append(ring_copy(slot, places, h, core))
            started[-1].start()

    def take(slot, part):
        ring_copy(slot, 2, 0, part).wait_recv()

    def split_k(i, carry):
        for q in range(4):
            pairs = []
            for s in (4 * q, 4 * q + 2):
                second = k_buf[i, s + 1] if s + 1 < 15 else jnp.zeros((64, 64), F32)
                pairs.append(jnp.concatenate([k_buf[i, s], second], axis=1))
            both = jnp.concatenate(pairs, axis=1)
            high = both.astype(BF16)
            lanes = slice(256 * q, 256 * q + 256)
            k_split[i, 0:64, lanes] = high
            k_split[i, 64:128, lanes] = (both - high.astype(F32)).astype(BF16)
        return carry

    def split_part(part):
        k_copies[part].wait()
        lax.fori_loop(4 * part, 4 * part + 4, split_k, 0, unroll=True)

    def place_group(side):
        def place(m, carry):
            tiles = [[near[side, n, m * 3 + u] for u in range(3)] for n in range(4)]
            turned = [[swap_rows(tile) for tile in each] for each in tiles]

            def piece(index, x, under):
                n, u = index // 5, index % 5 - side
                if u < 0 or u > 2:
                    return None
                return (tiles if x == under else turned)[n][u]

            for x in range(2):
                wholes = [[], []]
                for at in range(10):
                    upper, under = piece(2 * at, x, 0), piece(2 * at + 1, x, 1)
                    if upper is None and under is None:
                        wholes[0].append(jnp.zeros((8, 128), F32))
                        wholes[1].append(jnp.zeros((8, 128), F32))
                    else:
                        tile = jnp.where(top, 0.0 if upper is None else upper, 0.0 if under is None else under)
                        wholes[0].append(tile)
                        wholes[1].append(swap_lanes(tile))
                for flipped in range(2):
                    whole = jnp.concatenate(wholes[flipped], axis=0)
                    high = whole.astype(BF16)
                    entry_at = 8 * side + 4 * m + 2 * x + flipped
                    table[entry_at, 0] = high
                    table[entry_at, 1] = (whole - high.astype(F32)).astype(BF16)
            return carry

        lax.fori_loop(0, 2, place, 0, unroll=True)

    split_part(0)
    split_part(1)
    table[24:26] = jnp.zeros((2, 2, 80, 128), BF16)
    pair_copy(0, odd * 2 + 1 - core, core, pair_peers[0]).wait_recv()
    for n in range(2):
        pair_copy(0, (1 - odd) * 2 + n, core, pair_peers[0]).wait_recv()
    place_group(1)

    @pl.when(lower)
    def _():
        place_group(2)

    @pl.when(jnp.logical_not(lower))
    def _():
        place_group(0)

    def merge(zero, one):
        mixed = swap_rows(jnp.where(top, one, zero))
        return [jnp.where(top, zero, mixed), jnp.where(top, mixed, one)]

    def prepare(slot):
        def tile(part, at):
            return near[1, odd * 2 + part, at] if slot == 0 else ring[slot - 1, part, at]

        rows = []
        for u in range(3):
            pieces = merge(tile(0, u), tile(1, u)) + merge(tile(0, 3 + u), tile(1, 3 + u))
            rows.append(jnp.concatenate(pieces, axis=1))
        whole = jnp.concatenate(rows, axis=0)
        return jnp.concatenate([whole, whole - whole.astype(BF16).astype(F32)], axis=0).astype(BF16)

    own_factor = prepare(0)

    @pl.when(has_side)
    def _():
        for number in range(4):
            halo_take(number)

    @pl.when(lower)
    def _():
        place_group(0)

    @pl.when(jnp.logical_not(lower))
    def _():
        place_group(2)

    copies[2].wait()

    def entry(i, s):
        if s >= 15:
            return 24
        block = k_cols[AGG * core + i, s]
        place_of = block - (first_row + AGG * core - AGG)
        inside = (block >= 0) & (block < total_rows) & (place_of >= 0) & (place_of < 24)
        return jnp.where(inside, place_of, 24)

    low_16 = lax.broadcasted_iota(jnp.int32, (80, 128), 1) < 64
    blank = jnp.zeros((48, 128), BF16)

    def multiply_row(i):
        sides = []
        for s in range(0, 16, 2):
            even = entry(i, s)
            other = lax.bitwise_xor(entry(i, s + 1), 1)
            parts = [jnp.where(low_16, table[even, part], table[other, part]) for part in range(2)]
            sides.append(jnp.concatenate([parts[0], blank, parts[1], blank], axis=0))
        total = lax.dot_general(
            k_split[i],
            jnp.concatenate(sides, axis=1),
            (((1,), (1,)), ((), ())),
            preferred_element_type=F32,
        )
        return total[0:64, 0:128] + total[0:64, 128:256] + total[64:128, 0:128]

    def multiply(i, carry):
        rows = pl.ds(pl.multiple_of(64 * i, 64), 64)
        value = multiply_row(i)
        high = value.astype(BF16)
        weights[rows, 0:128] = high
        weights[rows, 128:256] = (value - high.astype(F32)).astype(BF16)
        return carry

    lax.fori_loop(0, AGG, multiply, 0, unroll=True)

    lane = lax.broadcasted_iota(jnp.int32, (8, 128), 1)
    lane_group = lane // 32

    def spread(value, u):
        start = 8 - 4 * u
        moved = [pltpu.roll(value, start + 12 * n, 1) if start + 12 * n else value for n in range(4)]
        first = jnp.where(lane_group == 0, moved[0], moved[1])
        second = jnp.where(lane_group == 2, moved[2], moved[3])
        within = lane % 32 - start
        return jnp.where((within >= 0) & (within < 20), jnp.where(lane < 64, first, second), 0.0)

    def products(slots, factors):
        result = lax.dot_general(
            jnp.concatenate(factors, axis=0),
            weights[...],
            (((1,), (0,)), ((), ())),
            preferred_element_type=F32,
        )
        for n, slot in enumerate(slots):
            for u in range(3):
                a = 48 * n + 8 * u
                value = result[a : a + 8, 0:128] + result[a : a + 8, 128:256] + result[a + 24 : a + 32, 0:128]
                terms[u, slot] = spread(value, u)

    factors = [own_factor]
    for slot in range(1, 4):
        for part in range(2):
            take(slot, part)
        factors.append(prepare(slot))
    products((0, 1, 2, 3), factors)

    def rotate(value, groups):
        return value if groups % 4 == 0 else pltpu.roll(value, 32 * (groups % 4), 1)

    def pack(u):
        parts = [terms[u, slot] for slot in range(4)]
        for number in range(4):
            moved = [rotate(parts[slot], slot - number) for slot in range(4)]
            left_half = jnp.where(lane_group == 0, moved[0], moved[1])
            right_half = jnp.where(lane_group == 2, moved[2], moved[3])
            packed[number, u] = jnp.where(low, left_half, right_half)

    pack(0)
    pack(2)

    def side_copy(number):
        return pltpu.make_async_remote_copy(
            src_ref=packed.at[number, 2 * core],
            dst_ref=side_in.at[odd, 1 - core],
            send_sem=side_send.at[number],
            recv_sem=side_recv.at[odd, 1 - core],
            device_id=member(side_row, number),
            device_id_type=MESH,
        )

    def side_take(n, block):
        pltpu.make_async_remote_copy(
            src_ref=packed.at[0, 0],
            dst_ref=side_in.at[n, block],
            send_sem=side_send.at[0],
            recv_sem=side_recv.at[n, block],
            device_id=member(row - 1 + 2 * block, 2 * n + 1 - block),
            device_id_type=MESH,
        ).wait_recv()

    @pl.when(has_side)
    def _():
        for number in range(4):
            side_copy(number).start()

    pack(1)

    def last_copy(n, number, chip, which, peer):
        return pltpu.make_async_remote_copy(
            src_ref=packed.at[number, pl.ds(1 - core, 2)],
            dst_ref=pair_in.at[chip, which],
            send_sem=pair_send.at[3 + n],
            recv_sem=last_recv.at[chip, which],
            device_id=peer,
            device_id_type=MESH,
        )

    for n, peer in enumerate(pair_peers):
        number = odd * 2 + 1 - core if n == 0 else (1 - odd) * 2 + n - 1
        started.append(last_copy(n, number, odd, core, peer))
        started[-1].start()
    pair_in[odd, core] = packed[me, pl.ds(1 - core, 2)]
    last_copy(0, 0, odd, 1 - core, pair_peers[0]).wait_recv()
    for n in range(2):
        last_copy(0, 0, 1 - odd, n, pair_peers[0]).wait_recv()

    @pl.when(has_below)
    def _():
        for n in range(2):
            side_take(n, 0)

    @pl.when(has_above)
    def _():
        for n in range(2):
            side_take(n, 1)

    for chip in range(2):
        totals = [pair_in[chip, 0, n] + pair_in[chip, 1, n] + side_in[chip, n] for n in range(2)]
        for slot in range(4):
            place_at = z - odd + chip + RING + (slot if chip else -slot)
            final[lax.rem(place_at, RING)] = jnp.where(
                lane_group == 0, rotate(totals[0], -slot), rotate(totals[1], 1 - slot)
            )
    turned = jnp.transpose(jnp.concatenate([final[n] for n in range(RING)], axis=0))
    for block in range(2):
        for band in range(7):
            a = 32 * block + 4 * band
            out[block, band] = turned[a : a + 4]

    for copy in started:
        copy.wait_send()

    @pl.when(has_below)
    def _():
        for n in range(2):
            halo_copy(0, n).wait_send()

    @pl.when(has_above)
    def _():
        for n in range(2):
            halo_copy(1, n).wait_send()

    @pl.when(has_side)
    def _():
        for number in range(4):
            side_copy(number).wait_send()


def body(row_count, k_vals, k_cols, p_vals, p_cols):
    own = k_vals.shape[0]
    dma = pltpu.SemaphoreType.DMA
    operands = [jnp.transpose(p_cols), k_cols, jnp.transpose(p_vals, (0, 1, 3, 2)), k_vals]
    result = pl.pallas_call(
        functools.partial(kernel, row_count),
        out_shape=jax.ShapeDtypeStruct((2, 7, 4, 64), F32),
        in_specs=[pl.BlockSpec(memory_space=pltpu.HBM)] * 4,
        out_specs=pl.BlockSpec(memory_space=pltpu.VMEM),
        scratch_shapes=[
            pltpu.SMEM((3, own), jnp.int32),
            pltpu.SMEM((own, 15), jnp.int32),
            pltpu.VMEM((own, 3, 4, 64), F32),
            pltpu.VMEM((AGG, 15, 64, 64), F32),
            pltpu.VMEM((AGG, 128, 1024), BF16),
            pltpu.VMEM((3, 4, 6, 8, 128), F32),
            pltpu.VMEM((3, 2, 6, 8, 128), F32),
            pltpu.VMEM((26, 2, 80, 128), BF16),
            pltpu.VMEM((512, 256), BF16),
            pltpu.VMEM((3, 4, 8, 128), F32),
            pltpu.VMEM((4, 3, 8, 128), F32),
            pltpu.VMEM((2, 2, 2, 8, 128), F32),
            pltpu.VMEM((2, 2, 8, 128), F32),
            pltpu.VMEM((RING, 8, 128), F32),
            dma((5,)),
            dma((3, 2)),
            dma((3, 2)),
            dma((6,)),
            dma((4,)),
            dma((2, 2)),
            dma((2, 2)),
            dma((4,)),
            dma((4,)),
            dma((2, 2)),
        ],
        compiler_params=pltpu.CompilerParams(
            collective_id=0, has_side_effects=True, vmem_limit_bytes=32 * 1024 * 1024
        ),
    )(*[pltpu.with_memory_space_constraint(operand, pltpu.HBM) for operand in operands])
    return jnp.transpose(result, (0, 1, 3, 2))


def solution(mesh):
    placed = (
        P("row", None, None, None),
        P("row", None),
        P("row", None, None, "col"),
        P("row", None),
    )
    return jax.shard_map(
        functools.partial(body, mesh.shape["row"]),
        mesh=mesh,
        in_specs=placed,
        out_specs=P("row", None, None, "col"),
        check_vma=False,
    )
```

```python
import functools

import jax
import jax.numpy as jnp
from jax import lax
from jax.experimental import pallas as pl
from jax.experimental.pallas import tpu as pltpu
from jax.sharding import PartitionSpec as P

AGG = 8
RING = 8
SPREAD = ((3, -3), (2, 2), (1, -1))
MESH = pl.DeviceIdType.MESH
F32 = jnp.float32
BF16 = jnp.bfloat16


def kernel(
    row_count,
    p_cols_hbm,
    k_cols_hbm,
    p_hbm,
    k_hbm,
    out,
    p_cols,
    k_cols,
    p_buf,
    k_buf,
    k_split,
    near,
    ring,
    table,
    weights,
    terms,
    packed,
    pair_in,
    side_in,
    final,
    local_sem,
    ring_send,
    ring_recv,
    pair_send,
    pair_recv,
    last_recv,
    halo_send,
    halo_recv,
    side_send,
    side_recv,
):
    row = lax.axis_index("row")
    col = lax.axis_index("col")
    z = lax.div(col, 2)
    core = lax.rem(col, 2)
    own_rows = 2 * AGG
    first_row = row * own_rows
    total_rows = row_count * own_rows
    blocks_all = total_rows // AGG
    has_above = row < row_count - 1
    has_below = row > 0
    lower = core == 0
    has_side = jnp.where(lower, row, row_count - 1 - row) > 0
    has_other = jnp.where(lower, row_count - 1 - row, row) > 0
    side_row = row - 1 + 2 * core
    other_row = row + 1 - 2 * core
    odd = lax.rem(z, 2)
    turn = 1 - 2 * odd
    me = odd * 2 + core

    def along(places, which):
        return (row, lax.rem(z + turn * places + RING, RING) * 2 + which)

    def member(at_row, number):
        return (at_row, (z - odd) * 2 + number)

    pair_peers = [(row, z * 2 + 1 - core), along(1, 0), along(1, 1)]

    copies = [
        pltpu.make_async_copy(p_hbm, p_buf, local_sem.at[0]),
        pltpu.make_async_copy(p_cols_hbm, p_cols, local_sem.at[1]),
        pltpu.make_async_copy(k_cols_hbm, k_cols, local_sem.at[2]),
    ]
    for copy in copies:
        copy.start()
    barrier = pltpu.get_barrier_semaphore()

    def greet(peer):
        pl.semaphore_signal(barrier, inc=1, device_id=peer, device_id_type=MESH)

    for peer in pair_peers:
        greet(peer)
    for places in (-1, 2, -2, -3):
        for which in range(2):
            greet(along(places, which))

    @pl.when(has_side)
    def _():
        for number in range(4):
            greet(member(side_row, number))

    @pl.when(has_other)
    def _():
        for n in range(2):
            greet(member(other_row, 2 * n + core))

    k_copies = []
    for part in range(2):
        k_copies.append(
            pltpu.make_async_copy(
                k_hbm.at[pl.ds(AGG * core + 4 * part, 4)], k_buf.at[pl.ds(4 * part, 4)], local_sem.at[3 + part]
            )
        )
        k_copies[-1].start()

    top = lax.broadcasted_iota(jnp.int32, (8, 128), 0) < 4
    low = lax.broadcasted_iota(jnp.int32, (8, 128), 1) < 64

    def swap_rows(value):
        return pltpu.roll(value, 4, 0)

    def swap_lanes(value):
        return pltpu.roll(value, 64, 1)

    copies[1].wait()
    copies[0].wait()

    def window(j, u):
        total = jnp.zeros((4, 64), F32)
        for t in range(3):
            block = p_cols[t, j]
            position = block - (2 * row + j // AGG) + 1
            position = jnp.where((block >= 0) & (block < blocks_all), position, -1)
            total = total + jnp.where(jnp.full((4, 64), position) == u, p_buf[j, t], 0.0)
        return total

    for h in range(2):
        for m in range(2):
            for u in range(3):
                halves = []
                for x in range(2):
                    j = AGG * h + 4 * m + 2 * x
                    halves.append(jnp.concatenate([window(j, u), window(j + 1, u)], axis=1))
                near[h + 1 - core, me, m * 3 + u] = jnp.concatenate(halves, axis=0)

    @pl.when(jnp.logical_not(has_side))
    def _():
        near[2 * core] = jnp.zeros((4, 6, 8, 128), F32)

    @pl.when(jnp.logical_not(has_below))
    def _():
        for n in range(2):
            side_in[n, 0] = jnp.zeros((8, 128), F32)

    @pl.when(jnp.logical_not(has_above))
    def _():
        for n in range(2):
            side_in[n, 1] = jnp.zeros((8, 128), F32)

    pl.semaphore_wait(barrier, jnp.where(has_side, 4, 0) + jnp.where(has_other, 2, 0) + 11)

    def pair_copy(n, number, which, peer):
        return pltpu.make_async_remote_copy(
            src_ref=near.at[pl.ds(1 - core, 2), number],
            dst_ref=near.at[pl.ds(1 - which, 2), number],
            send_sem=pair_send.at[n],
            recv_sem=pair_recv.at[number],
            device_id=peer,
            device_id_type=MESH,
        )

    started = []
    for n, peer in enumerate(pair_peers):
        started.append(pair_copy(n, me, 1 - core if n == 0 else n - 1, peer))
        started[-1].start()

    def halo_copy(h, n):
        return pltpu.make_async_remote_copy(
            src_ref=near.at[h + 1 - core, me],
            dst_ref=near.at[2 - 2 * h, me],
            send_sem=halo_send.at[h, n],
            recv_sem=halo_recv.at[me],
            device_id=member(row - 1 + 2 * h, 2 * n + 1 - h),
            device_id_type=MESH,
        )

    def halo_take(number):
        pltpu.make_async_remote_copy(
            src_ref=near.at[1, number],
            dst_ref=near.at[2 * core, number],
            send_sem=halo_send.at[0, 0],
            recv_sem=halo_recv.at[number],
            device_id=member(side_row, number),
            device_id_type=MESH,
        ).wait_recv()

    @pl.when(has_below)
    def _():
        for n in range(2):
            halo_copy(0, n).start()

    @pl.when(has_above)
    def _():
        for n in range(2):
            halo_copy(1, n).start()

    def ring_copy(slot, places, h, part):
        return pltpu.make_async_remote_copy(
            src_ref=near.at[h + 1 - core, me],
            dst_ref=ring.at[slot - 1, part],
            send_sem=ring_send.at[slot - 1, h],
            recv_sem=ring_recv.at[slot - 1, part],
            device_id=along(places, h),
            device_id_type=MESH,
        )

    for slot, places in SPREAD:
        for h in range(2):
            started.append(ring_copy(slot, places, h, core))
            started[-1].start()

    def take(slot, part):
        ring_copy(slot, 2, 0, part).wait_recv()

    def split_k(i, carry):
        for q in range(4):
            pairs = []
            for s in (4 * q, 4 * q + 2):
                second = k_buf[i, s + 1] if s + 1 < 15 else jnp.zeros((64, 64), F32)
                pairs.append(jnp.concatenate([k_buf[i, s], second], axis=1))
            both = jnp.concatenate(pairs, axis=1)
            high = both.astype(BF16)
            lanes = slice(256 * q, 256 * q + 256)
            k_split[i, 0:64, lanes] = high
            k_split[i, 64:128, lanes] = (both - high.astype(F32)).astype(BF16)
        return carry

    def split_part(part):
        k_copies[part].wait()
        lax.fori_loop(4 * part, 4 * part + 4, split_k, 0, unroll=True)

    def place_group(side):
        def place(m, carry):
            tiles = [[near[side, n, m * 3 + u] for u in range(3)] for n in range(4)]
            turned = [[swap_rows(tile) for tile in each] for each in tiles]

            def piece(index, x, under):
                n, u = index // 5, index % 5 - side
                if u < 0 or u > 2:
                    return None
                return (tiles if x == under else turned)[n][u]

            for x in range(2):
                wholes = [[], []]
                for at in range(10):
                    upper, under = piece(2 * at, x, 0), piece(2 * at + 1, x, 1)
                    if upper is None and under is None:
                        wholes[0].append(jnp.zeros((8, 128), F32))
                        wholes[1].append(jnp.zeros((8, 128), F32))
                    else:
                        tile = jnp.where(top, 0.0 if upper is None else upper, 0.0 if under is None else under)
                        wholes[0].append(tile)
                        wholes[1].append(swap_lanes(tile))
                for flipped in range(2):
                    whole = jnp.concatenate(wholes[flipped], axis=0)
                    high = whole.astype(BF16)
                    entry_at = 8 * side + 4 * m + 2 * x + flipped
                    table[entry_at, 0] = high
                    table[entry_at, 1] = (whole - high.astype(F32)).astype(BF16)
            return carry

        lax.fori_loop(0, 2, place, 0, unroll=True)

    split_part(0)
    split_part(1)
    table[24:26] = jnp.zeros((2, 2, 80, 128), BF16)
    pair_copy(0, odd * 2 + 1 - core, core, pair_peers[0]).wait_recv()
    for n in range(2):
        pair_copy(0, (1 - odd) * 2 + n, core, pair_peers[0]).wait_recv()
    place_group(1)

    @pl.when(lower)
    def _():
        place_group(2)

    @pl.when(jnp.logical_not(lower))
    def _():
        place_group(0)

    def merge(zero, one):
        mixed = swap_rows(jnp.where(top, one, zero))
        return [jnp.where(top, zero, mixed), jnp.where(top, mixed, one)]

    def prepare(slot):
        def tile(part, at):
            return near[1, odd * 2 + part, at] if slot == 0 else ring[slot - 1, part, at]

        rows = []
        for u in range(3):
            pieces = merge(tile(0, u), tile(1, u)) + merge(tile(0, 3 + u), tile(1, 3 + u))
            rows.append(jnp.concatenate(pieces, axis=1))
        whole = jnp.concatenate(rows, axis=0)
        return jnp.concatenate([whole, whole - whole.astype(BF16).astype(F32)], axis=0).astype(BF16)

    own_factor = prepare(0)

    @pl.when(has_side)
    def _():
        for number in range(4):
            halo_take(number)

    @pl.when(lower)
    def _():
        place_group(0)

    @pl.when(jnp.logical_not(lower))
    def _():
        place_group(2)

    copies[2].wait()

    def entry(i, s):
        if s >= 15:
            return 24
        block = k_cols[AGG * core + i, s]
        place_of = block - (first_row + AGG * core - AGG)
        inside = (block >= 0) & (block < total_rows) & (place_of >= 0) & (place_of < 24)
        return jnp.where(inside, place_of, 24)

    low_16 = lax.broadcasted_iota(jnp.int32, (80, 128), 1) < 64
    blank = jnp.zeros((48, 128), BF16)

    def multiply_row(i):
        sides = []
        for s in range(0, 16, 2):
            even = entry(i, s)
            other = lax.bitwise_xor(entry(i, s + 1), 1)
            parts = [jnp.where(low_16, table[even, part], table[other, part]) for part in range(2)]
            sides.append(jnp.concatenate([parts[0], blank, parts[1], blank], axis=0))
        total = lax.dot_general(
            k_split[i],
            jnp.concatenate(sides, axis=1),
            (((1,), (1,)), ((), ())),
            preferred_element_type=F32,
        )
        return total[0:64, 0:128] + total[0:64, 128:256] + total[64:128, 0:128]

    def multiply(i, carry):
        rows = pl.ds(pl.multiple_of(64 * i, 64), 64)
        value = multiply_row(i)
        high = value.astype(BF16)
        weights[rows, 0:128] = high
        weights[rows, 128:256] = (value - high.astype(F32)).astype(BF16)
        return carry

    lax.fori_loop(0, AGG, multiply, 0, unroll=True)

    lane = lax.broadcasted_iota(jnp.int32, (8, 128), 1)
    lane_group = lane // 32

    def spread(value, u):
        start = 8 - 4 * u
        moved = [pltpu.roll(value, start + 12 * n, 1) if start + 12 * n else value for n in range(4)]
        first = jnp.where(lane_group == 0, moved[0], moved[1])
        second = jnp.where(lane_group == 2, moved[2], moved[3])
        within = lane % 32 - start
        return jnp.where((within >= 0) & (within < 20), jnp.where(lane < 64, first, second), 0.0)

    def products(slots, factors):
        result = lax.dot_general(
            jnp.concatenate(factors, axis=0),
            weights[...],
            (((1,), (0,)), ((), ())),
            preferred_element_type=F32,
        )
        for n, slot in enumerate(slots):
            for u in range(3):
                a = 48 * n + 8 * u
                value = result[a : a + 8, 0:128] + result[a : a + 8, 128:256] + result[a + 24 : a + 32, 0:128]
                terms[u, slot] = spread(value, u)

    factors = [own_factor]
    for slot in range(1, 4):
        for part in range(2):
            take(slot, part)
        factors.append(prepare(slot))
    products((0, 1, 2, 3), factors)

    def rotate(value, groups):
        return value if groups % 4 == 0 else pltpu.roll(value, 32 * (groups % 4), 1)

    def pack(u):
        parts = [terms[u, slot] for slot in range(4)]
        for number in range(4):
            moved = [rotate(parts[slot], slot - number) for slot in range(4)]
            left_half = jnp.where(lane_group == 0, moved[0], moved[1])
            right_half = jnp.where(lane_group == 2, moved[2], moved[3])
            packed[number, u] = jnp.where(low, left_half, right_half)

    pack(0)
    pack(2)

    def side_copy(number):
        return pltpu.make_async_remote_copy(
            src_ref=packed.at[number, 2 * core],
            dst_ref=side_in.at[odd, 1 - core],
            send_sem=side_send.at[number],
            recv_sem=side_recv.at[odd, 1 - core],
            device_id=member(side_row, number),
            device_id_type=MESH,
        )

    def side_take(n, block):
        pltpu.make_async_remote_copy(
            src_ref=packed.at[0, 0],
            dst_ref=side_in.at[n, block],
            send_sem=side_send.at[0],
            recv_sem=side_recv.at[n, block],
            device_id=member(row - 1 + 2 * block, 2 * n + 1 - block),
            device_id_type=MESH,
        ).wait_recv()

    @pl.when(has_side)
    def _():
        for number in range(4):
            side_copy(number).start()

    pack(1)

    def last_copy(n, number, chip, which, peer):
        return pltpu.make_async_remote_copy(
            src_ref=packed.at[number, pl.ds(1 - core, 2)],
            dst_ref=pair_in.at[chip, which],
            send_sem=pair_send.at[3 + n],
            recv_sem=last_recv.at[chip, which],
            device_id=peer,
            device_id_type=MESH,
        )

    for n, peer in ((1, pair_peers[1]), (2, pair_peers[2]), (0, pair_peers[0])):
        number = odd * 2 + 1 - core if n == 0 else (1 - odd) * 2 + n - 1
        started.append(last_copy(n, number, odd, core, peer))
        started[-1].start()
    pair_in[odd, core] = packed[me, pl.ds(1 - core, 2)]
    last_copy(0, 0, odd, 1 - core, pair_peers[0]).wait_recv()
    for n in range(2):
        last_copy(0, 0, 1 - odd, n, pair_peers[0]).wait_recv()

    @pl.when(has_below)
    def _():
        for n in range(2):
            side_take(n, 0)

    @pl.when(has_above)
    def _():
        for n in range(2):
            side_take(n, 1)

    for chip in range(2):
        totals = [pair_in[chip, 0, n] + pair_in[chip, 1, n] + side_in[chip, n] for n in range(2)]
        for slot in range(4):
            place_at = z - odd + chip + RING + (slot if chip else -slot)
            final[lax.rem(place_at, RING)] = jnp.where(
                lane_group == 0, rotate(totals[0], -slot), rotate(totals[1], 1 - slot)
            )
    turned = jnp.transpose(jnp.concatenate([final[n] for n in range(RING)], axis=0))
    for block in range(2):
        for band in range(7):
            a = 32 * block + 4 * band
            out[block, band] = turned[a : a + 4]

    for copy in started:
        copy.wait_send()

    @pl.when(has_below)
    def _():
        for n in range(2):
            halo_copy(0, n).wait_send()

    @pl.when(has_above)
    def _():
        for n in range(2):
            halo_copy(1, n).wait_send()

    @pl.when(has_side)
    def _():
        for number in range(4):
            side_copy(number).wait_send()


def body(row_count, k_vals, k_cols, p_vals, p_cols):
    own = k_vals.shape[0]
    dma = pltpu.SemaphoreType.DMA
    operands = [jnp.transpose(p_cols), k_cols, jnp.transpose(p_vals, (0, 1, 3, 2)), k_vals]
    result = pl.pallas_call(
        functools.partial(kernel, row_count),
        out_shape=jax.ShapeDtypeStruct((2, 7, 4, 64), F32),
        in_specs=[pl.BlockSpec(memory_space=pltpu.HBM)] * 4,
        out_specs=pl.BlockSpec(memory_space=pltpu.VMEM),
        scratch_shapes=[
            pltpu.SMEM((3, own), jnp.int32),
            pltpu.SMEM((own, 15), jnp.int32),
            pltpu.VMEM((own, 3, 4, 64), F32),
            pltpu.VMEM((AGG, 15, 64, 64), F32),
            pltpu.VMEM((AGG, 128, 1024), BF16),
            pltpu.VMEM((3, 4, 6, 8, 128), F32),
            pltpu.VMEM((3, 2, 6, 8, 128), F32),
            pltpu.VMEM((26, 2, 80, 128), BF16),
            pltpu.VMEM((512, 256), BF16),
            pltpu.VMEM((3, 4, 8, 128), F32),
            pltpu.VMEM((4, 3, 8, 128), F32),
            pltpu.VMEM((2, 2, 2, 8, 128), F32),
            pltpu.VMEM((2, 2, 8, 128), F32),
            pltpu.VMEM((RING, 8, 128), F32),
            dma((5,)),
            dma((3, 2)),
            dma((3, 2)),
            dma((6,)),
            dma((4,)),
            dma((2, 2)),
            dma((2, 2)),
            dma((4,)),
            dma((4,)),
            dma((2, 2)),
        ],
        compiler_params=pltpu.CompilerParams(
            collective_id=0, has_side_effects=True, vmem_limit_bytes=32 * 1024 * 1024
        ),
    )(*[pltpu.with_memory_space_constraint(operand, pltpu.HBM) for operand in operands])
    return jnp.transpose(result, (0, 1, 3, 2))


def solution(mesh):
    placed = (
        P("row", None, None, None),
        P("row", None),
        P("row", None, None, "col"),
        P("row", None),
    )
    return jax.shard_map(
        functools.partial(body, mesh.shape["row"]),
        mesh=mesh,
        in_specs=placed,
        out_specs=P("row", None, None, "col"),
        check_vma=False,
    )
```
